512 devices in a mesh: section: 4 (over y), resp: 128 (over z, x, core).
Axes of the slice: x: 4, y: 4, z: 16, core: 2. Of those that a mesh axis runs over, the one named last changes fastest.
Arguments:
- queries: bfloat16 [4, 8192, 4096], P('section', 'resp'), may hold values from -100 to 100
- resp_kv: bfloat16 [4, 8192, 1024], P('section', 'resp'), may hold values from -4 to 4
- prefix_kv: bfloat16 [4, 65536, 1024], P('section', 'resp'), may hold values from -6 to 6
- owner: int32 [4, 4], P('section'), may hold values from 0 to 127, as said below
- seg_len: int32 [256, 4], P('resp'), may hold values from 1 to 16, 32 in all within a row
Outputs:
- out: bfloat16 [4, 8192, 4096], P('section', 'resp')
The draws below stay inside these ranges and needn't reach their ends.
Inputs may be any that keep to these rules, and one draw needn't show every extreme that they name: owner[l, p] is one of the devices p * 32 to (p + 1) * 32 - 1, those holding prompt p's responses.
All inputs are finite; a program needn't handle non-finite values.
Results may differ from the reference program's by a relative error of at most 0.0099.
Values may be sent and summed in bfloat16 or wider, within the bound.
No kernel may reach another device: no remote copies, remote signals or barrier semaphores. Data moves between devices by JAX's collectives and lax.ppermute only.
A program may use at most 64 MiB of HBM per device.

```python
import math
import jax
import jax.numpy as jnp
import numpy as np
from jax import lax

HQ = 32
KVH = 4
HEAD_SIZE = 128
PLEN = 512
TOKM = 32
MB = 2
RESPS = 4
PROMPTS = 4
KVW = 512
MOSTLEN = 16
LAYERS = 4
ROWS = 8192
N_RESP = 128


def common_parts(key):
    group_size = N_RESP // PROMPTS
    owner_ranks = jax.random.randint(jax.random.fold_in(key, 11), (LAYERS, PROMPTS), 0, group_size)
    owner_ranks = owner_ranks.at[0, 0].set(0).at[LAYERS - 1, PROMPTS - 1].set(group_size - 1)
    owners = owner_ranks + (jnp.arange(PROMPTS, dtype=jnp.int32) * group_size)[None, :]
    key_table = jnp.clip(jax.random.normal(jax.random.fold_in(key, 13), (LAYERS, N_RESP * PLEN, KVH * HEAD_SIZE), jnp.float32), -4.0, 4.0)
    return (owners.astype(jnp.int32), key_table)


def draw_owner(key, part):
    owners, key_table = common_parts(key)
    return owners


def draw_prefix_kv(key, part):
    owners, key_table = common_parts(key)
    key = jax.random.fold_in(key, 3)
    value_shape = (LAYERS, N_RESP * PLEN, KVH * HEAD_SIZE)
    values = jnp.clip(jax.random.normal(jax.random.fold_in(key, 2), value_shape, jnp.float32), -4.0, 4.0)
    return jnp.concatenate([key_table, values], axis=2).astype(jnp.bfloat16)


def draw_queries(key, part):
    key = jax.random.fold_in(key, 5)
    full_shape = (LAYERS, ROWS, HQ * HEAD_SIZE)
    return jnp.clip(jax.random.normal(key, full_shape, jnp.float32), -4.0, 4.0).astype(jnp.bfloat16)


def steps_of(stream_key, extent, cuts, least, largest):
    level, own = 1.0, jax.random.fold_in(stream_key, 6)
    for dim, shards_of in cuts:
        heights = jnp.exp(jax.random.uniform(jax.random.fold_in(own, dim), (shards_of,), jnp.float32, least / len(cuts), largest / len(cuts)))
        level = level * jnp.repeat(heights, extent[dim] // shards_of).reshape([-1 if axis == dim else 1 for axis in range(len(extent))])
    return level


def profile(number_of, total, most, slope):
    weights = [(1 << 20) // math.isqrt(grade ** slope) + 1 for grade in range(2, number_of + 1)]
    spare, holding = total - most - (number_of - 1), [1] * (number_of - 1)
    while spare > 0:
        candidates = [i for i in range(number_of - 1) if holding[i] < most]
        mass, remaining = sum([weights[i] for i in candidates]), spare
        for i in candidates:
            extra = min(most - holding[i], max(1, remaining * weights[i] // mass), spare)
            holding[i] = holding[i] + extra
            spare = spare - extra
    return np.array([most] + holding)


def uneven_parts(stream_key, count, total, bound, slope):
    if count == 2:
        one = jax.random.randint(stream_key, (), max(1, total - bound), min(bound, total - 1) + 1)
        return jnp.stack([one, total - one])
    sizes = jnp.asarray(profile(count, total, bound, slope), jnp.int32)
    couples = (count - 1) // 2
    giver, sink = sizes[1:1 + 2 * couples:2], sizes[2:2 + 2 * couples:2]
    slack = jnp.minimum(giver - 1, bound - sink)
    moved = jax.random.randint(jax.random.fold_in(stream_key, 1), (couples,), 0, 1 << 20) % (slack + 1)
    sizes = sizes.at[1:1 + 2 * couples:2].set(giver - moved).at[2:2 + 2 * couples:2].set(sink + moved)
    return sizes[jax.random.permutation(jax.random.fold_in(stream_key, 2), count)]


def normal_values(key, dims, scale, bound, pieces=(), kind=jnp.bfloat16):
    loudness = steps_of(key, dims, pieces, -0.22, 0.18) if pieces else 1.0
    drawn = jax.random.normal(key, dims, jnp.float32) * scale * loudness
    return jnp.minimum(jnp.maximum(drawn, -bound), bound).astype(kind)


def setup_inputs(seed: int = 0) -> dict:
    key_list = jax.random.split(jax.random.key(seed), 6)
    return {
        "queries": draw_queries(jax.random.fold_in(key_list[5], 71), 0),
        "resp_kv": normal_values(key_list[1], (LAYERS, ROWS, 2 * KVW), 1.0, 4.0, ((0, 4), (1, 128))),
        "prefix_kv": draw_prefix_kv(jax.random.fold_in(key_list[5], 71), 0),
        "owner": draw_owner(jax.random.fold_in(key_list[5], 71), 0),
        "seg_len": jax.vmap(lambda own: uneven_parts(own, RESPS, TOKM, MOSTLEN, 2))(jax.random.split(key_list[4], (N_RESP * MB))).reshape((N_RESP * MB, RESPS)).astype(jnp.int32),
    }


EPS = 1e-06

def same_response(lengths, count_of_rows):
    ends = jnp.cumsum(lengths).astype(jnp.int32)
    position = jnp.arange(count_of_rows, dtype=jnp.int32)
    response = lax.optimization_barrier(jnp.sum((position[:, None] >= ends[None, :]).astype(jnp.int32), axis=1)).astype(jnp.int32)
    return (response[:, None] == response[None, :]) & (position[None, :] <= position[:, None])

def attend(mixed, prefix, local_rows, local_lengths):
    count_of_rows = mixed.shape[0]
    kv_width = prefix.shape[1] // 2
    groups = kv_width // HEAD_SIZE
    joined = jnp.concatenate([prefix, local_rows], axis=0)
    key_matrix = joined[:, :kv_width].reshape(-1, groups, HEAD_SIZE).astype(jnp.float32)
    value_matrix = joined[:, kv_width:].reshape(-1, groups, HEAD_SIZE).astype(jnp.float32)
    heads_of_query = mixed.reshape(count_of_rows, groups, HQ // groups, HEAD_SIZE).astype(jnp.float32)
    logit_scores = jnp.einsum('fiqv,civ->iqfc', heads_of_query, key_matrix) * (1.0 / math.sqrt(HEAD_SIZE))
    allowed = jnp.concatenate([jnp.ones((count_of_rows, prefix.shape[0]), bool), same_response(local_lengths, count_of_rows)], axis=1)
    logit_scores = jnp.where(allowed[None, None], logit_scores, -jnp.inf)
    row_top = lax.optimization_barrier(jnp.max(logit_scores, axis=3, keepdims=True))
    expo = jnp.exp(logit_scores - row_top)
    softmax_weights = (expo / lax.optimization_barrier(jnp.sum(expo, axis=3, keepdims=True))).astype(jnp.bfloat16)
    attended_output = jnp.einsum('euzm,meh->zeuh', softmax_weights.astype(jnp.float32), value_matrix).reshape(count_of_rows, -1)
    square = lax.optimization_barrier(jnp.mean(attended_output * attended_output, axis=1, keepdims=True))
    return (attended_output * lax.rsqrt(square + EPS)).astype(jnp.bfloat16)

def reference(queries, resp_kv, prefix_kv, owner, seg_len):
    group_size = N_RESP // PROMPTS
    lengths = seg_len.reshape(N_RESP, MB, RESPS)
    carried = jnp.zeros((N_RESP, MB, TOKM, HQ * HEAD_SIZE), jnp.bfloat16)
    outputs = []
    for layer_index in range(LAYERS):
        layer_queries = queries[layer_index].reshape(N_RESP, MB, TOKM, -1)
        layer_local = resp_kv[layer_index].reshape(N_RESP, MB, TOKM, -1)
        prefix_slots = prefix_kv[layer_index].reshape(N_RESP, PLEN, -1)
        owner_row = owner[layer_index]

        def per_device(packed_args):
            device_index, query_dev, local_dev, carry_dev, length_dev = packed_args
            root_owner = owner_row[device_index // group_size].astype(jnp.int32)
            prefix = lax.dynamic_index_in_dim(prefix_slots, root_owner, 0, keepdims=False)

            def per_micro(inner_args):
                query_rows, local_rows, carry_rows, local_lengths = inner_args
                mixed = (query_rows.astype(jnp.float32) + carry_rows.astype(jnp.float32)).astype(jnp.bfloat16)
                return attend(mixed, prefix, local_rows, local_lengths)
            return lax.map(per_micro, (query_dev, local_dev, carry_dev, length_dev))
        result = lax.map(per_device, (jnp.arange(N_RESP, dtype=jnp.int32), layer_queries, layer_local, carried, lengths))
        outputs.append(result.reshape(N_RESP * MB * TOKM, -1))
        carried = result
    return jnp.stack(outputs)
```

```python
import math

import jax
import jax.numpy as jnp
from jax import lax
from jax.experimental import pallas as pl
from jax.experimental.pallas import tpu as pltpu
from jax.sharding import Mesh, PartitionSpec as P

HQ = 32
KVH = 4
GROUP = HQ // KVH
HEAD_SIZE = 128
WIDTH = HQ * HEAD_SIZE
KVW = KVH * HEAD_SIZE
PLEN = 512
TOKM = 32
RESPS = 4
PROMPTS = 4
EPS = 1e-06
EXP2_SCALE = math.log2(math.e) / math.sqrt(HEAD_SIZE)

SECTION = ("yh", "yl")
RESP = ("p", "zh", "zl", "x", "c")
PLANE = ("zl", "x")
SPREAD = ("yl", *PLANE)


def swap(x, axis):
    return lax.ppermute(x, axis, [(0, 1), (1, 0)])


def product(a, b, over):
    return lax.dot_general(a, b, (((over,), (over,)), ((), ())), preferred_element_type=jnp.float32)


def over_rows(reduce, blocks):
    pair = jnp.maximum if reduce is jnp.max else jnp.add
    wide = reduce(pair(blocks[0], blocks[1]), axis=0, keepdims=True)
    return pair(wide, reduce(blocks[2], axis=0, keepdims=True))


def attend(x, keys, values, near_mask, att_ref):
    rows = x.shape[0]
    groups = range(KVH)
    heads = [x[:, h * HEAD_SIZE : (h + 1) * HEAD_SIZE] for h in range(HQ)]
    queries = [jnp.concatenate(heads[g * GROUP : (g + 1) * GROUP], axis=0) for g in groups]
    scores = [[product(k, queries[g], 1) for k in keys(g)] for g in groups]
    for g in groups:
        scores[g][2] = scores[g][2] + near_mask
    top = [over_rows(jnp.max, scores[g]) for g in groups]
    raised = [[jnp.exp2((s - top[g]) * EXP2_SCALE) for s in scores[g]] for g in groups]
    share = [1.0 / over_rows(jnp.sum, raised[g]) for g in groups]
    weights = [[(e * share[g]).astype(jnp.bfloat16) for e in raised[g]] for g in groups]
    total = jnp.zeros((1, GROUP * rows), jnp.float32)
    for g in groups:
        out = sum(product(v, w, 0) for v, w in zip(values(g), weights[g], strict=True))
        att_ref[g] = out
        total = total + jnp.sum(out * out, axis=0, keepdims=True)
    reach = rows
    while reach < GROUP * rows:
        total = total + pltpu.roll(total, reach, 1)
        reach *= 2
    return lax.rsqrt(total * (1.0 / WIDTH) + EPS)


def pair_kernel(place_ref, seg_ref, own_ref, other_ref, *refs):
    if len(refs) == 6:
        carried_ref, kv0_ref, kv1_ref, a_ref, b_ref, att_ref = refs
        carried = carried_ref[...].astype(jnp.float32)
    else:
        kv0_ref, kv1_ref, b_ref, a_ref, att_ref = refs
        carried = 0.0
    micro, second = place_ref[0], place_ref[1]

    at_key = lax.broadcasted_iota(jnp.int32, (TOKM, TOKM), 0)
    at_query = lax.broadcasted_iota(jnp.int32, (TOKM, TOKM), 1)
    of_key, of_query = jnp.zeros_like(at_key), jnp.zeros_like(at_query)
    end = jnp.int32(0)
    for i in range(RESPS):
        end = end + seg_ref[micro, i]
        of_key = of_key + (at_key >= end).astype(jnp.int32)
        of_query = of_query + (at_query >= end).astype(jnp.int32)
    allowed = (of_key == of_query) & (at_key <= at_query)
    near_mask = jnp.where(allowed, 0.0, -jnp.inf).astype(jnp.float32)
    near_mask = jnp.concatenate([near_mask] * GROUP, axis=1)

    for layer, out_ref in enumerate((a_ref, b_ref)):
        is_own = second == layer
        query = jnp.where(is_own, own_ref[:, :WIDTH], other_ref[:, :WIDTH]).astype(jnp.float32)
        near = jnp.where(is_own, own_ref[:, WIDTH:], other_ref[:, WIDTH:])
        x = (query + carried).astype(jnp.bfloat16)

        def blocks(first, layer=layer, near=near):
            def of_group(g):
                lanes = slice(first + g * HEAD_SIZE, first + (g + 1) * HEAD_SIZE)
                return [kv0_ref[layer, :, lanes], kv1_ref[layer, :, lanes], near[:, lanes]]

            return of_group

        scaling = attend(x, blocks(0), blocks(KVW), near_mask, att_ref)
        for g in range(KVH):
            normed = (att_ref[g] * scaling).T.astype(jnp.bfloat16)
            for at in range(GROUP):
                h = g * GROUP + at
                out_ref[:, h * HEAD_SIZE : (h + 1) * HEAD_SIZE] = normed[at * TOKM : (at + 1) * TOKM]
        if layer == 0:
            carried = a_ref[...].astype(jnp.float32)


def attend_pair(place, seg_len, own, other, carried, kv0, kv1):
    vmem = pl.BlockSpec(memory_space=pltpu.VMEM)
    smem = pl.BlockSpec(memory_space=pltpu.SMEM)
    out = jax.ShapeDtypeStruct((TOKM, WIDTH), jnp.bfloat16)
    scratch = [pltpu.VMEM((KVH, HEAD_SIZE, GROUP * TOKM), jnp.float32)]
    if carried is None:
        middle, outs, scratch = [], (out,), [pltpu.VMEM(out.shape, out.dtype), *scratch]
    else:
        middle, outs = [carried], (out, out)
    return pl.pallas_call(
        pair_kernel,
        out_shape=outs,
        in_specs=[smem, smem] + [vmem] * (4 + len(middle)),
        out_specs=(vmem,) * len(outs),
        scratch_shapes=scratch,
        compiler_params=pltpu.CompilerParams(vmem_limit_bytes=12 * 1024 * 1024),
        cost_estimate=pl.CostEstimate(
            flops=2 * 4 * HQ * TOKM * (PLEN + TOKM) * HEAD_SIZE,
            bytes_accessed=4 * 1024 * 1024,
            transcendentals=2 * HQ * TOKM * (PLEN + TOKM),
        ),
    )(place, seg_len, own, other, *middle, kv0, kv1)


def spread_prefix(prefix, is_owner, is_other_core, beside):
    half = PLEN // 2
    parts = math.prod(lax.axis_size(axis) for axis in PLANE)
    arrived = swap(prefix, "c")
    zero = jnp.zeros((), jnp.bfloat16)
    mine = jnp.where(is_owner, prefix[:half], jnp.where(is_other_core, arrived[half:], zero))
    pieces = lax.all_to_all(mine.reshape(parts, half // parts, -1), PLANE, 0, 0)
    piece = jnp.sum(pieces, axis=0)
    piece = piece + swap(piece, "zh")
    piece, beside = lax.optimization_barrier((piece, beside))
    copies = lax.axis_size("yl") * parts
    gathered = lax.all_to_all(jnp.broadcast_to(piece[None], (copies, *piece.shape)), SPREAD, 0, 0)
    gathered = gathered.reshape(lax.axis_size("yl"), -1, gathered.shape[2])
    return gathered, swap(gathered, "c"), beside


def local(queries, resp_kv, prefix_kv, owner, seg_len):
    at = {axis: lax.axis_index(axis) for axis in SECTION + RESP}
    place = jnp.int32(0)
    for axis in RESP:
        place = place * lax.axis_size(axis) + at[axis]
    owner_here = lax.dynamic_index_in_dim(owner[0], at["p"], 0, keepdims=False)
    micro = at["yl"] ^ at["yh"]
    where = jnp.stack([micro, at["yl"]]).astype(jnp.int32)

    def rows_of(which):
        arrays = (queries[0], resp_kv[0])
        return jnp.concatenate(
            [lax.dynamic_slice_in_dim(a, which * TOKM, TOKM, 0) for a in arrays], axis=1
        )

    own, theirs = rows_of(micro), rows_of(1 - micro)
    other = swap(theirs, "yl")
    kv0, kv1, other = spread_prefix(
        prefix_kv[0], owner_here == place, owner_here == (place ^ 1), other
    )

    fixed = (where, seg_len, own, other)
    (second,) = attend_pair(*fixed, None, kv0, kv1)
    carried = lax.ppermute(second, SECTION, [(0, 3), (1, 2)])
    first, second = attend_pair(*fixed, carried, kv0, kv1)

    is_second = at["yl"] == 1
    kept = jnp.where(is_second, second, first)
    got = swap(jnp.where(is_second, first, second), "yl")
    low = jnp.where(micro == 0, kept, got)
    high = jnp.where(micro == 0, got, kept)
    return jnp.concatenate([low, high], axis=0)[None]


def solution(mesh):
    fine = Mesh(mesh.devices.reshape(2, 2, PROMPTS, 2, 2, 4, 2), SECTION + RESP)
    return jax.shard_map(
        local,
        mesh=fine,
        in_specs=(
            P(SECTION, RESP, None),
            P(SECTION, RESP, None),
            P(SECTION, RESP, None),
            P(SECTION, None),
            P(RESP, None),
        ),
        out_specs=P(SECTION, RESP, None),
        check_vma=False,
    )
```

```python
import math

import jax
import jax.numpy as jnp
from jax import lax
from jax.experimental import pallas as pl
from jax.experimental.pallas import tpu as pltpu
from jax.sharding import Mesh, PartitionSpec as P

HQ = 32
KVH = 4
GROUP = HQ // KVH
HEAD_SIZE = 128
WIDTH = HQ * HEAD_SIZE
KVW = KVH * HEAD_SIZE
PLEN = 512
TOKM = 32
RESPS = 4
PROMPTS = 4
EPS = 1e-06
EXP2_SCALE = math.log2(math.e) / math.sqrt(HEAD_SIZE)

SECTION = ("yh", "yl")
RESP = ("p", "zh", "zl", "x", "c")
PLANE = ("zl", "x")
SPREAD = ("yl", *PLANE)


def swap(x, axis):
    return lax.ppermute(x, axis, [(0, 1), (1, 0)])


def product(a, b, over):
    return lax.dot_general(a, b, (((over,), (over,)), ((), ())), preferred_element_type=jnp.float32)


def over_rows(reduce, blocks):
    pair = jnp.maximum if reduce is jnp.max else jnp.add
    wide = reduce(pair(blocks[0], blocks[1]), axis=0, keepdims=True)
    return pair(wide, reduce(blocks[2], axis=0, keepdims=True))


def attend(x, keys, values, near_mask, att_ref):
    rows = x.shape[0]
    groups = range(KVH)
    heads = [x[:, h * HEAD_SIZE : (h + 1) * HEAD_SIZE] for h in range(HQ)]
    queries = [jnp.concatenate(heads[g * GROUP : (g + 1) * GROUP], axis=0) for g in groups]
    scores = [[product(k, queries[g], 1) for k in keys(g)] for g in groups]
    for g in groups:
        scores[g][2] = scores[g][2] + near_mask
    top = [over_rows(jnp.max, scores[g]) for g in groups]
    raised = [[jnp.exp2((s - top[g]) * EXP2_SCALE) for s in scores[g]] for g in groups]
    share = [1.0 / over_rows(jnp.sum, raised[g]) for g in groups]
    weights = [[(e * share[g]).astype(jnp.bfloat16) for e in raised[g]] for g in groups]
    total = jnp.zeros((1, GROUP * rows), jnp.float32)
    for g in groups:
        out = sum(product(v, w, 0) for v, w in zip(values(g), weights[g], strict=True))
        att_ref[g] = out
        total = total + jnp.sum(out * out, axis=0, keepdims=True)
    reach = rows
    while reach < GROUP * rows:
        total = total + pltpu.roll(total, reach, 1)
        reach *= 2
    return lax.rsqrt(total * (1.0 / WIDTH) + EPS)


def place_in_pair():
    second = lax.axis_index("yl")
    return second ^ lax.axis_index("yh"), second


def pair_kernel(seg_ref, own_ref, other_ref, *refs):
    if len(refs) == 6:
        carried_ref, kv0_ref, kv1_ref, a_ref, b_ref, att_ref = refs
        carried = carried_ref[...].astype(jnp.float32)
    else:
        kv0_ref, kv1_ref, b_ref, a_ref, att_ref = refs
        carried = 0.0
    micro, second = place_in_pair()

    at_key = lax.broadcasted_iota(jnp.int32, (TOKM, TOKM), 0)
    at_query = lax.broadcasted_iota(jnp.int32, (TOKM, TOKM), 1)
    of_key, of_query = jnp.zeros_like(at_key), jnp.zeros_like(at_query)
    lengths = seg_ref[pl.ds(micro, 1), :]
    end = jnp.zeros((1, 1), jnp.int32)
    for i in range(RESPS):
        end = end + lengths[:, i : i + 1]
        of_key = of_key + (at_key >= end).astype(jnp.int32)
        of_query = of_query + (at_query >= end).astype(jnp.int32)
    allowed = (of_key == of_query) & (at_key <= at_query)
    near_mask = jnp.where(allowed, 0.0, -jnp.inf).astype(jnp.float32)
    near_mask = jnp.concatenate([near_mask] * GROUP, axis=1)

    for layer, out_ref in enumerate((a_ref, b_ref)):
        is_own = second == layer
        query = jnp.where(is_own, own_ref[:, :WIDTH], other_ref[:, :WIDTH]).astype(jnp.float32)
        near = jnp.where(is_own, own_ref[:, WIDTH:], other_ref[:, WIDTH:])
        x = (query + carried).astype(jnp.bfloat16)

        def blocks(first, layer=layer, near=near):
            def of_group(g):
                lanes = slice(first + g * HEAD_SIZE, first + (g + 1) * HEAD_SIZE)
                return [kv0_ref[layer, :, lanes], kv1_ref[layer, :, lanes], near[:, lanes]]

            return of_group

        scaling = attend(x, blocks(0), blocks(KVW), near_mask, att_ref)
        for g in range(KVH):
            normed = (att_ref[g] * scaling).T.astype(jnp.bfloat16)
            for at in range(GROUP):
                h = g * GROUP + at
                out_ref[:, h * HEAD_SIZE : (h + 1) * HEAD_SIZE] = normed[at * TOKM : (at + 1) * TOKM]
        if layer == 0:
            carried = a_ref[...].astype(jnp.float32)


def attend_pair(seg_len, own, other, carried, kv0, kv1):
    vmem = pl.BlockSpec(memory_space=pltpu.VMEM)
    out = jax.ShapeDtypeStruct((TOKM, WIDTH), jnp.bfloat16)
    scratch = [pltpu.VMEM((KVH, HEAD_SIZE, GROUP * TOKM), jnp.float32)]
    if carried is None:
        middle, outs, scratch = [], (out,), [pltpu.VMEM(out.shape, out.dtype), *scratch]
    else:
        middle, outs = [carried], (out, out)
    return pl.pallas_call(
        pair_kernel,
        out_shape=outs,
        in_specs=[vmem] * (5 + len(middle)),
        out_specs=(vmem,) * len(outs),
        scratch_shapes=scratch,
        compiler_params=pltpu.CompilerParams(vmem_limit_bytes=12 * 1024 * 1024),
        cost_estimate=pl.CostEstimate(
            flops=2 * 4 * HQ * TOKM * (PLEN + TOKM) * HEAD_SIZE,
            bytes_accessed=4 * 1024 * 1024,
            transcendentals=2 * HQ * TOKM * (PLEN + TOKM),
        ),
    )(seg_len, own, other, *middle, kv0, kv1)


def spread_prefix(prefix, is_owner, is_other_core, beside):
    half = PLEN // 2
    parts = math.prod(lax.axis_size(axis) for axis in PLANE)
    arrived = swap(prefix[half:], "c")
    zero = jnp.zeros((), jnp.bfloat16)
    mine = jnp.where(is_owner, prefix[:half], jnp.where(is_other_core, arrived, zero))
    pieces = lax.all_to_all(mine.reshape(parts, half // parts, -1), PLANE, 0, 0)
    piece = jnp.sum(pieces, axis=0)
    piece = piece + swap(piece, "zh")
    piece, beside = lax.optimization_barrier((piece, beside))
    copies = lax.axis_size("yl") * parts
    gathered = lax.all_to_all(jnp.broadcast_to(piece[None], (copies, *piece.shape)), SPREAD, 0, 0)
    gathered = gathered.reshape(lax.axis_size("yl"), -1, gathered.shape[2])
    return gathered, swap(gathered, "c"), beside


def local(queries, resp_kv, prefix_kv, owner, seg_len):
    at = {axis: lax.axis_index(axis) for axis in SECTION + RESP}
    place = jnp.int32(0)
    for axis in RESP:
        place = place * lax.axis_size(axis) + at[axis]
    owner_here = lax.dynamic_index_in_dim(owner[0], at["p"], 0, keepdims=False)
    micro, second = place_in_pair()

    def rows_of(which):
        arrays = (queries[0], resp_kv[0])
        return jnp.concatenate(
            [lax.dynamic_slice_in_dim(a, which * TOKM, TOKM, 0) for a in arrays], axis=1
        )

    own, theirs = rows_of(micro), rows_of(1 - micro)
    other = swap(theirs, "yl")
    kv0, kv1, other = spread_prefix(
        prefix_kv[0], owner_here == place, owner_here == (place ^ 1), other
    )

    fixed = (seg_len, own, other)
    (last,) = attend_pair(*fixed, None, kv0, kv1)
    carried = lax.ppermute(last, SECTION, [(0, 3), (1, 2)])
    first, last = attend_pair(*fixed, carried, kv0, kv1)

    kept = jnp.where(second == 1, last, first)
    got = swap(jnp.where(second == 1, first, last), "yl")
    low = jnp.where(micro == 0, kept, got)
    high = jnp.where(micro == 0, got, kept)
    return jnp.concatenate([low, high], axis=0)[None]


def solution(mesh):
    fine = Mesh(mesh.devices.reshape(2, 2, PROMPTS, 2, 2, 4, 2), SECTION + RESP)
    return jax.shard_map(
        local,
        mesh=fine,
        in_specs=(
            P(SECTION, RESP, None),
            P(SECTION, RESP, None),
            P(SECTION, RESP, None),
            P(SECTION, None),
            P(RESP, None),
        ),
        out_specs=P(SECTION, RESP, None),
        check_vma=False,
    )
```

```python
import functools
import math

import jax
import jax.numpy as jnp
from jax import lax
from jax.experimental import pallas as pl
from jax.experimental.pallas import tpu as pltpu
from jax.sharding import Mesh, PartitionSpec as P

HQ = 32
KVH = 4
GROUP = HQ // KVH
HEAD_SIZE = 128
WIDTH = HQ * HEAD_SIZE
KVW = KVH * HEAD_SIZE
PLEN = 512
TOKM = 32
RESPS = 4
PROMPTS = 4
EPS = 1e-06
EXP2_SCALE = math.log2(math.e) / math.sqrt(HEAD_SIZE)

SECTION = ("yh", "yl")
RESP = ("p", "zh", "zl", "x", "c")
PLANE = ("zl", "x", "c")
SPREAD = ("yl", "zl", "x")


def swap(x, axis):
    return lax.ppermute(x, axis, [(0, 1), (1, 0)])


def product(a, b, over):
    return lax.dot_general(a, b, (((over,), (over,)), ((), ())), preferred_element_type=jnp.float32)


def over_rows(reduce, blocks):
    pair = jnp.maximum if reduce is jnp.max else jnp.add
    wide = reduce(pair(blocks[0], blocks[1]), axis=0, keepdims=True)
    return pair(wide, reduce(blocks[2], axis=0, keepdims=True))


def attend(x, keys, values, near_mask, att_ref):
    rows = x.shape[0]
    groups = range(KVH)
    heads = [x[:, h * HEAD_SIZE : (h + 1) * HEAD_SIZE] for h in range(HQ)]
    queries = [jnp.concatenate(heads[g * GROUP : (g + 1) * GROUP], axis=0) for g in groups]
    scores = [[product(k, queries[g], 1) for k in keys(g)] for g in groups]
    for g in groups:
        scores[g][2] = scores[g][2] + near_mask
    top = [over_rows(jnp.max, scores[g]) for g in groups]
    raised = [[jnp.exp2((s - top[g]) * EXP2_SCALE) for s in scores[g]] for g in groups]
    share = [1.0 / over_rows(jnp.sum, raised[g]) for g in groups]
    weights = [[(e * share[g]).astype(jnp.bfloat16) for e in raised[g]] for g in groups]
    total = jnp.zeros((1, GROUP * rows), jnp.float32)
    for g in groups:
        out = sum(product(v, w, 0) for v, w in zip(values(g), weights[g], strict=True))
        att_ref[g] = out
        total = total + jnp.sum(out * out, axis=0, keepdims=True)
    reach = rows
    while reach < GROUP * rows:
        total = total + pltpu.roll(total, reach, 1)
        reach *= 2
    return lax.rsqrt(total * (1.0 / WIDTH) + EPS)


def pair_kernel(micro, seg_ref, q_ref, rkv_ref, other_ref, *refs):
    carried = 0.0
    done_ref = None
    if len(refs) == 4:
        kv0_ref, kv1_ref, out_ref, att_ref = refs
    elif len(refs) == 5:
        carried_ref, kv0_ref, kv1_ref, out_ref, att_ref = refs
    else:
        carried_ref, done_ref, kv0_ref, kv1_ref, out_ref, att_ref = refs
    ends = len(refs) > 4
    if ends:
        carried = carried_ref[...].astype(jnp.float32)
    second = lax.axis_index("yl")
    rows = slice(micro * TOKM, (micro + 1) * TOKM)

    at_key = lax.broadcasted_iota(jnp.int32, (TOKM, TOKM), 0)
    at_query = lax.broadcasted_iota(jnp.int32, (TOKM, TOKM), 1)
    of_key, of_query = jnp.zeros_like(at_key), jnp.zeros_like(at_query)
    end = jnp.zeros((1, 1), jnp.int32)
    for i in range(RESPS):
        end = end + seg_ref[micro : micro + 1, i : i + 1]
        of_key = of_key + (at_key >= end).astype(jnp.int32)
        of_query = of_query + (at_query >= end).astype(jnp.int32)
    allowed = (of_key == of_query) & (at_key <= at_query)
    near_mask = jnp.where(allowed, 0.0, -jnp.inf).astype(jnp.float32)
    near_mask = jnp.concatenate([near_mask] * GROUP, axis=1)

    outs = []
    for layer in range(2):
        is_own = second == layer
        query = jnp.where(is_own, q_ref[rows, :], other_ref[rows, :WIDTH]).astype(jnp.float32)
        near = jnp.where(is_own, rkv_ref[rows, :], other_ref[rows, WIDTH:])
        x = (query + carried).astype(jnp.bfloat16)

        def blocks(first, layer=layer, near=near):
            def of_group(g):
                lanes = slice(first + g * HEAD_SIZE, first + (g + 1) * HEAD_SIZE)
                return [kv0_ref[layer, :, lanes], kv1_ref[layer, :, lanes], near[:, lanes]]

            return of_group

        scaling = attend(x, blocks(0), blocks(KVW), near_mask, att_ref)
        heads = []
        for g in range(KVH):
            normed = (att_ref[g] * scaling).T.astype(jnp.bfloat16)
            heads += [normed[at * TOKM : (at + 1) * TOKM] for at in range(GROUP)]
        outs.append(jnp.concatenate(heads, axis=1))
        carried = outs[0].astype(jnp.float32)
    result = jnp.where(second == 0, outs[0], outs[1]) if ends else outs[1]
    if done_ref is None:
        out_ref[...] = result
    else:
        out_ref[:TOKM] = done_ref[...]
        out_ref[TOKM:] = result


def attend_pair(micro, fixed, kv, carried=None, done=None):
    vmem = pl.BlockSpec(memory_space=pltpu.VMEM)
    rows = TOKM if done is None else 2 * TOKM
    middle = [x for x in (carried, done) if x is not None]
    return pl.pallas_call(
        functools.partial(pair_kernel, micro),
        out_shape=jax.ShapeDtypeStruct((rows, WIDTH), jnp.bfloat16),
        in_specs=[vmem] * (len(fixed) + len(middle) + len(kv)),
        out_specs=vmem,
        scratch_shapes=[pltpu.VMEM((KVH, HEAD_SIZE, GROUP * TOKM), jnp.float32)],
        compiler_params=pltpu.CompilerParams(vmem_limit_bytes=12 * 1024 * 1024),
        cost_estimate=pl.CostEstimate(
            flops=2 * 4 * HQ * TOKM * (PLEN + TOKM) * HEAD_SIZE,
            bytes_accessed=4 * 1024 * 1024,
            transcendentals=2 * HQ * TOKM * (PLEN + TOKM),
        ),
    )(*fixed, *middle, *kv)


def spread_prefix(prefix, owner_piece, in_half, beside):
    parts = math.prod(lax.axis_size(axis) for axis in PLANE)
    pieces = lax.all_to_all(prefix.reshape(parts, PLEN // parts, -1), PLANE, 0, 0)
    piece = lax.dynamic_index_in_dim(pieces, owner_piece, 0, keepdims=False)
    piece = jnp.where(in_half, piece, swap(piece, "zh"))
    piece, beside = lax.optimization_barrier((piece, beside))
    copies = math.prod(lax.axis_size(axis) for axis in SPREAD)
    gathered = lax.all_to_all(jnp.broadcast_to(piece[None], (copies, *piece.shape)), SPREAD, 0, 0)
    gathered = gathered.reshape(lax.axis_size("yl"), -1, gathered.shape[2])
    return gathered, swap(gathered, "c"), beside


def local(queries, resp_kv, prefix_kv, owner, seg_len):
    at = {axis: lax.axis_index(axis) for axis in ("p", "zh")}
    owner_rank = jnp.sum(jnp.where(jnp.arange(PROMPTS) == at["p"], owner[0], 0))
    parts = math.prod(lax.axis_size(axis) for axis in PLANE)
    owner_piece = owner_rank % parts
    in_half = owner_rank // parts % lax.axis_size("zh") == at["zh"]

    other = swap(jnp.concatenate([queries[0], resp_kv[0]], axis=1), "yl")
    kv0, kv1, other = spread_prefix(prefix_kv[0], owner_piece, in_half, other)

    fixed, kv = (seg_len, queries[0], resp_kv[0], other), (kv0, kv1)
    hop = [(0, 3), (1, 2)]
    carried0 = lax.ppermute(attend_pair(0, fixed, kv), SECTION, hop)
    carried1 = lax.ppermute(attend_pair(1, fixed, kv), SECTION, hop)
    done = attend_pair(0, fixed, kv, carried0)
    return attend_pair(1, fixed, kv, carried1, done)[None]


def solution(mesh):
    fine = Mesh(mesh.devices.reshape(2, 2, PROMPTS, 2, 2, 4, 2), SECTION + RESP)
    return jax.shard_map(
        local,
        mesh=fine,
        in_specs=(
            P(SECTION, RESP, None),
            P(SECTION, RESP, None),
            P(SECTION, RESP, None),
            P(SECTION, None),
            P(RESP, None),
        ),
        out_specs=P(SECTION, RESP, None),
        check_vma=False,
    )
```

```python
import functools
import math

import jax
import jax.numpy as jnp
from jax import lax
from jax.experimental import pallas as pl
from jax.experimental.pallas import tpu as pltpu
from jax.sharding import Mesh, PartitionSpec as P

HQ = 32
KVH = 4
GROUP = HQ // KVH
HEAD_SIZE = 128
WIDTH = HQ * HEAD_SIZE
KVW = KVH * HEAD_SIZE
PLEN = 512
TOKM = 32
MB = 2
LANES = GROUP * TOKM
EARLY = 6
RESPS = 4
PROMPTS = 4
EPS = 1e-06
EXP2_SCALE = math.log2(math.e) / math.sqrt(HEAD_SIZE)

SECTION = ("yh", "yl")
RESP = ("p", "zh", "zl", "x", "c")
PLANE = ("zl", "x")
SPREAD = ("yl", *PLANE)


def swap(x, axis):
    return lax.ppermute(x, axis, [(0, 1), (1, 0)])


def product(a, b, a_over, b_over):
    over = (((a_over,), (b_over,)), ((), ()))
    return lax.dot_general(a, b, over, preferred_element_type=jnp.float32)


def over_rows(reduce, blocks):
    pair = jnp.maximum if reduce is jnp.max else jnp.add
    wide = reduce(pair(blocks[0], blocks[1]), axis=0, keepdims=True)
    return pair(wide, reduce(blocks[2], axis=0, keepdims=True))


def attend(x, keys, values, near_mask, att_ref):
    groups = range(KVH)
    lanes = x[0].shape[1]
    scores = [[product(k, x[g], 1, 0) for k in keys(g)] for g in groups]
    for g in groups:
        scores[g][2] = scores[g][2] + near_mask
    top = [over_rows(jnp.max, scores[g]) for g in groups]
    raised = [[jnp.exp2((s - top[g]) * EXP2_SCALE) for s in scores[g]] for g in groups]
    share = [1.0 / over_rows(jnp.sum, raised[g]) for g in groups]
    weights = [[(e * share[g]).astype(jnp.bfloat16) for e in raised[g]] for g in groups]
    total = jnp.zeros((1, lanes), jnp.float32)
    for g in groups:
        out = sum(product(v, w, 0, 0) for v, w in zip(values(g), weights[g], strict=True))
        att_ref[g] = out
        total = total + jnp.sum(out * out, axis=0, keepdims=True)
    reach = TOKM
    while reach < lanes:
        total = total + pltpu.roll(total, reach, 1)
        reach *= 2
    scaling = lax.rsqrt(total * (1.0 / WIDTH) + EPS)
    return [(att_ref[g] * scaling).astype(jnp.bfloat16) for g in groups]


def pack_kernel(q_ref, rkv_ref, early_ref, late_ref):
    for micro in range(MB):
        rows = slice(micro * TOKM, (micro + 1) * TOKM)
        for g in range(KVH):
            heads = [
                q_ref[rows, h * HEAD_SIZE : (h + 1) * HEAD_SIZE]
                for h in range(g * GROUP, (g + 1) * GROUP)
            ]
            is_late, first = query_rows(micro, g)
            out_ref = late_ref if is_late else early_ref
            out_ref[first : first + HEAD_SIZE] = jnp.concatenate(heads, axis=0).T
        for part in range(2 * KVW // LANES):
            first = near_rows(micro, part)
            early_ref[first : first + TOKM] = rkv_ref[rows, part * LANES : (part + 1) * LANES]


def query_rows(micro, g):
    place = micro * KVH + g
    is_late = place >= EARLY
    return is_late, (place - EARLY if is_late else place) * HEAD_SIZE


def near_rows(micro, part):
    return EARLY * HEAD_SIZE + (micro * (2 * KVW // LANES) + part) * TOKM


def packed(q, rkv):
    vmem = pl.BlockSpec(memory_space=pltpu.VMEM)
    sizes = near_rows(MB, 0), (MB * KVH - EARLY) * HEAD_SIZE
    return pl.pallas_call(
        pack_kernel,
        out_shape=tuple(jax.ShapeDtypeStruct((size, LANES), jnp.bfloat16) for size in sizes),
        in_specs=[vmem, vmem],
        out_specs=(vmem, vmem),
        compiler_params=pltpu.CompilerParams(vmem_limit_bytes=12 * 1024 * 1024),
        cost_estimate=pl.CostEstimate(flops=0, bytes_accessed=1280 * 1024, transcendentals=0),
    )(q, rkv)


def pair_kernel(micro, seg_ref, own_ref, other_ref, *refs):
    late_refs, carried_ref, done_ref = (), None, None
    if micro == 1:
        *late_refs, refs = refs[0], refs[1], refs[2:]
    if len(refs) == 4:
        kv0_ref, kv1_ref, out_ref, att_ref = refs
    elif len(refs) == 5:
        carried_ref, kv0_ref, kv1_ref, out_ref, att_ref = refs
    else:
        carried_ref, done_ref, kv0_ref, kv1_ref, out_ref, att_ref, rows_ref, sems = refs
        copies = [
            pltpu.make_async_copy(source, out_ref.at[pl.ds(i * TOKM, TOKM)], sems.at[i])
            for i, source in enumerate((done_ref, rows_ref))
        ]
        copies[0].start()
    second = lax.axis_index("yl")

    at_key = lax.broadcasted_iota(jnp.int32, (TOKM, TOKM), 0)
    at_query = lax.broadcasted_iota(jnp.int32, (TOKM, TOKM), 1)
    of_key, of_query = jnp.zeros_like(at_key), jnp.zeros_like(at_query)
    end = jnp.zeros((1, 1), jnp.int32)
    for i in range(RESPS):
        end = end + seg_ref[micro : micro + 1, i : i + 1]
        of_key = of_key + (at_key >= end).astype(jnp.int32)
        of_query = of_query + (at_query >= end).astype(jnp.int32)
    allowed = (of_key == of_query) & (at_key <= at_query)
    near_mask = jnp.where(allowed, 0.0, -jnp.inf).astype(jnp.float32)
    near_mask = jnp.concatenate([near_mask] * GROUP, axis=1)

    def group_rows(g):
        return slice(g * HEAD_SIZE, (g + 1) * HEAD_SIZE)

    outs = []
    for layer in range(2):
        is_own = second == layer

        def one_of_both(first, count, lanes=slice(None), refs=(own_ref, other_ref), is_own=is_own):
            own, other = (ref[first : first + count, lanes] for ref in refs)
            return jnp.where(is_own, own, other)

        x = []
        for g in range(KVH):
            is_late, first = query_rows(micro, g)
            early = own_ref, other_ref
            query = one_of_both(first, HEAD_SIZE, refs=late_refs if is_late else early)
            if layer == 1:
                query = query.astype(jnp.float32) + outs[0][g].astype(jnp.float32)
            elif carried_ref is not None:
                query = query.astype(jnp.float32) + carried_ref[group_rows(g)].astype(jnp.float32)
            x.append(query.astype(jnp.bfloat16))

        def blocks(column, layer=layer, one_of_both=one_of_both):
            def of_group(g):
                lanes = slice(column + g * HEAD_SIZE, column + (g + 1) * HEAD_SIZE)
                first = near_rows(micro, lanes.start // LANES)
                inside = slice(lanes.start % LANES, lanes.start % LANES + HEAD_SIZE)
                near = one_of_both(first, TOKM, inside)
                return [kv0_ref[layer, :, lanes], kv1_ref[layer, :, lanes], near]

            return of_group

        outs.append(attend(x, blocks(0), blocks(KVW), near_mask, att_ref))
    if carried_ref is None:
        for g in range(KVH):
            out_ref[group_rows(g)] = outs[1][g]
        return
    if done_ref is None:
        rows_ref = out_ref
    for g in range(KVH):
        normed = jnp.where(second == 0, outs[0][g], outs[1][g]).T
        for at in range(GROUP):
            h = g * GROUP + at
            rows_ref[:, h * HEAD_SIZE : (h + 1) * HEAD_SIZE] = normed[at * TOKM : (at + 1) * TOKM]
    if done_ref is not None:
        copies[1].start()
        copies[0].wait()
        copies[1].wait()


def attend_pair(micro, fixed, kv, carried=None, done=None):
    vmem = pl.BlockSpec(memory_space=pltpu.VMEM)
    middle = [x for x in (carried, done) if x is not None]
    scratch = [pltpu.VMEM((KVH, HEAD_SIZE, LANES), jnp.float32)]
    shape, out_spec = (TOKM, WIDTH), vmem
    if carried is None:
        shape = (KVH * HEAD_SIZE, LANES)
    elif done is not None:
        shape, out_spec = (MB * TOKM, WIDTH), pl.BlockSpec(memory_space=pl.ANY)
        scratch += [pltpu.VMEM((TOKM, WIDTH), jnp.bfloat16), pltpu.SemaphoreType.DMA((2,))]
    return pl.pallas_call(
        functools.partial(pair_kernel, micro),
        out_shape=jax.ShapeDtypeStruct(shape, jnp.bfloat16),
        in_specs=[vmem] * (len(fixed) + len(middle) + len(kv)),
        out_specs=out_spec,
        scratch_shapes=scratch,
        compiler_params=pltpu.CompilerParams(vmem_limit_bytes=12 * 1024 * 1024),
        cost_estimate=pl.CostEstimate(
            flops=2 * 4 * HQ * TOKM * (PLEN + TOKM) * HEAD_SIZE,
            bytes_accessed=4 * 1024 * 1024,
            transcendentals=2 * HQ * TOKM * (PLEN + TOKM),
        ),
    )(*fixed, *middle, *kv)


def spread_prefix(prefix, is_owner, is_other_core, beside):
    half = PLEN // 2
    parts = math.prod(lax.axis_size(axis) for axis in PLANE)
    arrived = swap(prefix[half:], "c")
    zero = jnp.zeros((), jnp.bfloat16)
    mine = jnp.where(is_owner, prefix[:half], jnp.where(is_other_core, arrived, zero))
    pieces = lax.all_to_all(mine.reshape(parts, half // parts, -1), PLANE, 0, 0)
    piece = jnp.sum(pieces, axis=0)
    piece = piece + swap(piece, "zh")
    piece, beside = lax.optimization_barrier((piece, beside))
    copies = lax.axis_size("yl") * parts
    gathered = lax.all_to_all(jnp.broadcast_to(piece[None], (copies, *piece.shape)), SPREAD, 0, 0)
    gathered = gathered.reshape(lax.axis_size("yl"), -1, gathered.shape[2])
    return gathered, swap(gathered, "c"), beside


def local(queries, resp_kv, prefix_kv, owner, seg_len):
    at = {axis: lax.axis_index(axis) for axis in RESP}
    place = jnp.int32(0)
    for axis in RESP:
        place = place * lax.axis_size(axis) + at[axis]
    owner_here = lax.dynamic_index_in_dim(owner[0], at["p"], 0, keepdims=False)

    early, late = packed(queries[0], resp_kv[0])
    *kv, early_other = spread_prefix(
        prefix_kv[0], owner_here == place, owner_here == (place ^ 1), swap(early, "yl")
    )

    fixed = [(seg_len, early, early_other)]
    fixed.append((*fixed[0], late, swap(late, "yl")))
    hop = [(0, 3), (1, 2)]
    carried = [lax.ppermute(attend_pair(m, fixed[m], kv), SECTION, hop) for m in range(MB)]
    done = attend_pair(0, fixed[0], kv, carried[0])
    return attend_pair(1, fixed[1], kv, carried[1], done)[None]


def solution(mesh):
    fine = Mesh(mesh.devices.reshape(2, 2, PROMPTS, 2, 2, 4, 2), SECTION + RESP)
    return jax.shard_map(
        local,
        mesh=fine,
        in_specs=(
            P(SECTION, RESP, None),
            P(SECTION, RESP, None),
            P(SECTION, RESP, None),
            P(SECTION, None),
            P(RESP, None),
        ),
        out_specs=P(SECTION, RESP, None),
        check_vma=False,
    )
```

```python
import functools
import math

import jax
import jax.numpy as jnp
from jax import lax
from jax.experimental import pallas as pl
from jax.experimental.pallas import tpu as pltpu
from jax.sharding import Mesh, PartitionSpec as P

HQ = 32
KVH = 4
GROUP = HQ // KVH
HEAD_SIZE = 128
WIDTH = HQ * HEAD_SIZE
KVW = KVH * HEAD_SIZE
PLEN = 512
TOKM = 32
MB = 2
LANES = GROUP * TOKM
EARLY = 6
RESPS = 4
PROMPTS = 4
EPS = 1e-06
EXP2_SCALE = math.log2(math.e) / math.sqrt(HEAD_SIZE)

SECTION = ("yh", "yl")
RESP = ("p", "zh", "zl", "x", "c")
PLANE = ("zl", "x")
SPREAD = ("yl", *PLANE)


def swap(x, axis):
    return lax.ppermute(x, axis, [(0, 1), (1, 0)])


def product(a, b, a_over, b_over):
    over = (((a_over,), (b_over,)), ((), ()))
    return lax.dot_general(a, b, over, preferred_element_type=jnp.float32)


def over_rows(reduce, blocks):
    pair = jnp.maximum if reduce is jnp.max else jnp.add
    wide = reduce(pair(blocks[0], blocks[1]), axis=0, keepdims=True)
    return pair(wide, reduce(blocks[2], axis=0, keepdims=True))


def attend(x, keys, values, near_mask, att_ref):
    groups = range(KVH)
    lanes = x[0].shape[1]
    scores = [[product(k, x[g], 1, 0) for k in keys(g)] for g in groups]
    for g in groups:
        scores[g][2] = scores[g][2] + near_mask
    top = [over_rows(jnp.max, scores[g]) for g in groups]
    raised = [[jnp.exp2((s - top[g]) * EXP2_SCALE) for s in scores[g]] for g in groups]
    share = [1.0 / over_rows(jnp.sum, raised[g]) for g in groups]
    weights = [[(e * share[g]).astype(jnp.bfloat16) for e in raised[g]] for g in groups]
    total = jnp.zeros((1, lanes), jnp.float32)
    for g in groups:
        out = sum(product(v, w, 0, 0) for v, w in zip(values(g), weights[g], strict=True))
        att_ref[g] = out
        total = total + jnp.sum(out * out, axis=0, keepdims=True)
    reach = TOKM
    while reach < lanes:
        total = total + pltpu.roll(total, reach, 1)
        reach *= 2
    scaling = lax.rsqrt(total * (1.0 / WIDTH) + EPS)
    return [(att_ref[g] * scaling).astype(jnp.bfloat16) for g in groups]


def pack_kernel(q_ref, rkv_ref, early_ref, late_ref):
    for micro in range(MB):
        rows = slice(micro * TOKM, (micro + 1) * TOKM)
        for g in range(KVH):
            heads = [
                q_ref[rows, h * HEAD_SIZE : (h + 1) * HEAD_SIZE]
                for h in range(g * GROUP, (g + 1) * GROUP)
            ]
            is_late, first = query_rows(micro, g)
            out_ref = late_ref if is_late else early_ref
            out_ref[first : first + HEAD_SIZE] = jnp.concatenate(heads, axis=0).T
        for part in range(2 * KVW // LANES):
            first = near_rows(micro, part)
            early_ref[first : first + TOKM] = rkv_ref[rows, part * LANES : (part + 1) * LANES]


def query_rows(micro, g):
    place = micro * KVH + g
    is_late = place >= EARLY
    return is_late, (place - EARLY if is_late else place) * HEAD_SIZE


def near_rows(micro, part):
    return EARLY * HEAD_SIZE + (micro * (2 * KVW // LANES) + part) * TOKM


def packed(q, rkv):
    vmem = pl.BlockSpec(memory_space=pltpu.VMEM)
    sizes = near_rows(MB, 0), (MB * KVH - EARLY) * HEAD_SIZE
    return pl.pallas_call(
        pack_kernel,
        out_shape=tuple(jax.ShapeDtypeStruct((size, LANES), jnp.bfloat16) for size in sizes),
        in_specs=[vmem, vmem],
        out_specs=(vmem, vmem),
        compiler_params=pltpu.CompilerParams(vmem_limit_bytes=12 * 1024 * 1024),
        cost_estimate=pl.CostEstimate(flops=0, bytes_accessed=1280 * 1024, transcendentals=0),
    )(q, rkv)


def pair_kernel(micro, *refs):
    pair_body(micro, *refs)


def first_pair_kernel(micro, *refs):
    pl.when(lax.axis_index("yh") == 0)(functools.partial(pair_body, micro, *refs))


def pair_body(micro, seg_ref, own_ref, other_ref, *refs):
    late_refs, carried_ref, done_ref = (), None, None
    if micro == 1:
        *late_refs, refs = refs[0], refs[1], refs[2:]
    if len(refs) == 4:
        kv0_ref, kv1_ref, out_ref, att_ref = refs
    elif len(refs) == 5:
        carried_ref, kv0_ref, kv1_ref, out_ref, att_ref = refs
    else:
        carried_ref, done_ref, kv0_ref, kv1_ref, out_ref, att_ref, rows_ref, sems = refs
        copies = [
            pltpu.make_async_copy(source, out_ref.at[pl.ds(i * TOKM, TOKM)], sems.at[i])
            for i, source in enumerate((done_ref, rows_ref))
        ]
        copies[0].start()
    second = lax.axis_index("yl")

    at_key = lax.broadcasted_iota(jnp.int32, (TOKM, TOKM), 0)
    at_query = lax.broadcasted_iota(jnp.int32, (TOKM, TOKM), 1)
    of_key, of_query = jnp.zeros_like(at_key), jnp.zeros_like(at_query)
    end = jnp.zeros((1, 1), jnp.int32)
    for i in range(RESPS):
        end = end + seg_ref[micro : micro + 1, i : i + 1]
        of_key = of_key + (at_key >= end).astype(jnp.int32)
        of_query = of_query + (at_query >= end).astype(jnp.int32)
    allowed = (of_key == of_query) & (at_key <= at_query)
    near_mask = jnp.where(allowed, 0.0, -jnp.inf).astype(jnp.float32)
    near_mask = jnp.concatenate([near_mask] * GROUP, axis=1)

    def group_rows(g):
        return slice(g * HEAD_SIZE, (g + 1) * HEAD_SIZE)

    outs = []
    for layer in range(2):
        is_own = second == layer

        def one_of_both(first, count, lanes=slice(None), refs=(own_ref, other_ref), is_own=is_own):
            own, other = (ref[first : first + count, lanes] for ref in refs)
            return jnp.where(is_own, own, other)

        x = []
        for g in range(KVH):
            is_late, first = query_rows(micro, g)
            early = own_ref, other_ref
            query = one_of_both(first, HEAD_SIZE, refs=late_refs if is_late else early)
            if layer == 1:
                query = query.astype(jnp.float32) + outs[0][g].astype(jnp.float32)
            elif carried_ref is not None:
                query = query.astype(jnp.float32) + carried_ref[group_rows(g)].astype(jnp.float32)
            x.append(query.astype(jnp.bfloat16))

        def blocks(column, layer=layer, one_of_both=one_of_both):
            def of_group(g):
                lanes = slice(column + g * HEAD_SIZE, column + (g + 1) * HEAD_SIZE)
                first = near_rows(micro, lanes.start // LANES)
                inside = slice(lanes.start % LANES, lanes.start % LANES + HEAD_SIZE)
                near = one_of_both(first, TOKM, inside)
                return [kv0_ref[layer, :, lanes], kv1_ref[layer, :, lanes], near]

            return of_group

        outs.append(attend(x, blocks(0), blocks(KVW), near_mask, att_ref))
    if carried_ref is None:
        for g in range(KVH):
            out_ref[group_rows(g)] = outs[1][g]
        return
    if done_ref is None:
        rows_ref = out_ref
    for g in range(KVH):
        normed = jnp.where(second == 0, outs[0][g], outs[1][g]).T
        for at in range(GROUP):
            h = g * GROUP + at
            rows_ref[:, h * HEAD_SIZE : (h + 1) * HEAD_SIZE] = normed[at * TOKM : (at + 1) * TOKM]
    if done_ref is not None:
        copies[1].start()
        copies[0].wait()
        copies[1].wait()


def attend_pair(micro, fixed, kv, carried=None, done=None):
    vmem = pl.BlockSpec(memory_space=pltpu.VMEM)
    middle = [x for x in (carried, done) if x is not None]
    scratch = [pltpu.VMEM((KVH, HEAD_SIZE, LANES), jnp.float32)]
    shape, out_spec = (TOKM, WIDTH), vmem
    if carried is None:
        shape = (KVH * HEAD_SIZE, LANES)
    elif done is not None:
        shape, out_spec = (MB * TOKM, WIDTH), pl.BlockSpec(memory_space=pl.ANY)
        scratch += [pltpu.VMEM((TOKM, WIDTH), jnp.bfloat16), pltpu.SemaphoreType.DMA((2,))]
    return pl.pallas_call(
        functools.partial(first_pair_kernel if carried is None else pair_kernel, micro),
        out_shape=jax.ShapeDtypeStruct(shape, jnp.bfloat16),
        in_specs=[vmem] * (len(fixed) + len(middle) + len(kv)),
        out_specs=out_spec,
        scratch_shapes=scratch,
        compiler_params=pltpu.CompilerParams(vmem_limit_bytes=12 * 1024 * 1024),
        cost_estimate=pl.CostEstimate(
            flops=2 * 4 * HQ * TOKM * (PLEN + TOKM) * HEAD_SIZE,
            bytes_accessed=4 * 1024 * 1024,
            transcendentals=2 * HQ * TOKM * (PLEN + TOKM),
        ),
    )(*fixed, *middle, *kv)


def spread_prefix(prefix, is_owner, is_other_core, beside):
    half = PLEN // 2
    parts = math.prod(lax.axis_size(axis) for axis in PLANE)
    arrived = swap(prefix[half:], "c")
    zero = jnp.zeros((), jnp.bfloat16)
    mine = jnp.where(is_owner, prefix[:half], jnp.where(is_other_core, arrived, zero))
    pieces = lax.all_to_all(mine.reshape(parts, half // parts, -1), PLANE, 0, 0)
    piece = jnp.sum(pieces, axis=0)
    piece = piece + swap(piece, "zh")
    piece, beside = lax.optimization_barrier((piece, beside))
    copies = lax.axis_size("yl") * parts
    gathered = lax.all_to_all(jnp.broadcast_to(piece[None], (copies, *piece.shape)), SPREAD, 0, 0)
    gathered = gathered.reshape(lax.axis_size("yl"), -1, gathered.shape[2])
    return gathered, swap(gathered, "c"), beside


def local(queries, resp_kv, prefix_kv, owner, seg_len):
    at = {axis: lax.axis_index(axis) for axis in RESP}
    place = jnp.int32(0)
    for axis in RESP:
        place = place * lax.axis_size(axis) + at[axis]
    owner_here = lax.dynamic_index_in_dim(owner[0], at["p"], 0, keepdims=False)

    early, late = packed(queries[0], resp_kv[0])
    *kv, early_other = spread_prefix(
        prefix_kv[0], owner_here == place, owner_here == (place ^ 1), swap(early, "yl")
    )

    fixed = [(seg_len, early, early_other)]
    fixed.append((*fixed[0], late, swap(late, "yl")))
    hop = [(0, 3), (1, 2)]
    carried = [lax.ppermute(attend_pair(m, fixed[m], kv), SECTION, hop) for m in range(MB)]
    done = attend_pair(0, fixed[0], kv, carried[0])
    return attend_pair(1, fixed[1], kv, carried[1], done)[None]


def solution(mesh):
    fine = Mesh(mesh.devices.reshape(2, 2, PROMPTS, 2, 2, 4, 2), SECTION + RESP)
    return jax.shard_map(
        local,
        mesh=fine,
        in_specs=(
            P(SECTION, RESP, None),
            P(SECTION, RESP, None),
            P(SECTION, RESP, None),
            P(SECTION, None),
            P(RESP, None),
        ),
        out_specs=P(SECTION, RESP, None),
        check_vma=False,
    )
```

```python
import functools
import math

import jax
import jax.numpy as jnp
from jax import lax
from jax.experimental import pallas as pl
from jax.experimental.pallas import tpu as pltpu
from jax.sharding import Mesh, PartitionSpec as P

HQ = 32
KVH = 4
GROUP = HQ // KVH
HEAD_SIZE = 128
WIDTH = HQ * HEAD_SIZE
KVW = KVH * HEAD_SIZE
PLEN = 512
TOKM = 32
MB = 2
LANES = GROUP * TOKM
CHUNKS = 2 * KVW // LANES
PARTS = ((0, 0, 32), (1, 0, 16), (1, 16, 16))
RESPS = 4
PROMPTS = 4
EPS = 1e-06
EXP2_SCALE = math.log2(math.e) / math.sqrt(HEAD_SIZE)

SECTION = ("yh", "yl")
RESP = ("p", "zh", "zl", "x", "c")
PLANE = ("zl", "x")
SPREAD = ("yl", *PLANE)


def swap(x, axis):
    return lax.ppermute(x, axis, [(0, 1), (1, 0)])


def product(a, b, a_over, b_over):
    over = (((a_over,), (b_over,)), ((), ()))
    return lax.dot_general(a, b, over, preferred_element_type=jnp.float32)


def over_rows(reduce, blocks):
    pair = jnp.maximum if reduce is jnp.max else jnp.add
    wide = reduce(pair(blocks[0], blocks[1]), axis=0, keepdims=True)
    return pair(wide, reduce(blocks[2], axis=0, keepdims=True))


def over_heads(total, widths):
    sums, first = [], 0
    for width in widths:
        part = total[:, first : first + width]
        reach = width // GROUP
        while reach < width:
            part = part + pltpu.roll(part, reach, 1)
            reach *= 2
        sums.append(part)
        first += width
    return jnp.concatenate(sums, axis=1)


def attend(x, widths, keys, values, near_mask, att_ref):
    groups = range(KVH)
    lanes = x[0].shape[1]
    scores = [[product(k, x[g], 1, 0) for k in keys(g)] for g in groups]
    for g in groups:
        scores[g][2] = scores[g][2] + near_mask
    top = [over_rows(jnp.max, scores[g]) for g in groups]
    raised = [[jnp.exp2((s - top[g]) * EXP2_SCALE) for s in scores[g]] for g in groups]
    share = [1.0 / over_rows(jnp.sum, raised[g]) for g in groups]
    weights = [[(e * share[g]).astype(jnp.bfloat16) for e in raised[g]] for g in groups]
    total = jnp.zeros((1, lanes), jnp.float32)
    for g in groups:
        out = sum(product(v, w, 0, 0) for v, w in zip(values(g), weights[g], strict=True))
        att_ref[g] = out
        total = total + jnp.sum(out * out, axis=0, keepdims=True)
    scaling = lax.rsqrt(over_heads(total, widths) * (1.0 / WIDTH) + EPS)
    return [(att_ref[g] * scaling).astype(jnp.bfloat16) for g in groups]


def pack_kernel(q_ref, rkv_ref, early_ref, late_ref):
    for part, (micro, first, count) in enumerate(PARTS):
        out_ref = late_ref if part == len(PARTS) - 1 else early_ref
        rows = pl.ds(micro * TOKM + first, count)
        for g in range(KVH):
            heads = [
                q_ref[rows, h * HEAD_SIZE : (h + 1) * HEAD_SIZE]
                for h in range(g * GROUP, (g + 1) * GROUP)
            ]
            out_ref[query_block(part, g)] = jnp.concatenate(heads, axis=0).T
    for micro in range(MB):
        rows = pl.ds(micro * TOKM, TOKM)
        for chunk in range(CHUNKS):
            early_ref[near_block(micro, chunk)] = rkv_ref[rows, chunk * LANES : (chunk + 1) * LANES]


def query_block(part, g):
    lanes = GROUP * PARTS[part][2]
    beside = LANES // lanes
    first = 0
    if part < len(PARTS) - 1:
        first = sum(KVH * GROUP * count * HEAD_SIZE // LANES for _, _, count in PARTS[:part])
    first += g // beside * HEAD_SIZE
    lane = g % beside * lanes
    return slice(first, first + HEAD_SIZE), slice(lane, lane + lanes)


def near_block(micro, chunk):
    first = query_block(len(PARTS) - 2, KVH - 1)[0].stop + (micro * CHUNKS + chunk) * TOKM
    return slice(first, first + TOKM), slice(None)


def packed(q, rkv):
    vmem = pl.BlockSpec(memory_space=pltpu.VMEM)
    sizes = near_block(MB - 1, CHUNKS - 1)[0].stop, query_block(len(PARTS) - 1, KVH - 1)[0].stop
    return pl.pallas_call(
        pack_kernel,
        out_shape=tuple(jax.ShapeDtypeStruct((size, LANES), jnp.bfloat16) for size in sizes),
        in_specs=[vmem, vmem],
        out_specs=(vmem, vmem),
        compiler_params=pltpu.CompilerParams(vmem_limit_bytes=12 * 1024 * 1024),
        cost_estimate=pl.CostEstimate(flops=0, bytes_accessed=1280 * 1024, transcendentals=0),
    )(q, rkv)


def pair_kernel(parts, hopped, ready, seg_ref, own_ref, other_ref, *refs):
    micro = PARTS[parts[0]][0]
    widths = [GROUP * PARTS[part][2] for part in parts]
    late_refs = ()
    if micro > 0:
        late_refs, refs = refs[:2], refs[2:]
    second, pair = lax.axis_index("yl"), lax.axis_index("yh")

    def group_rows(g):
        return slice(g * HEAD_SIZE, (g + 1) * HEAD_SIZE)

    def both_layers(carried_ref, kv0_ref, kv1_ref, att_ref):
        at_key = lax.broadcasted_iota(jnp.int32, (TOKM, sum(widths)), 0)
        at_query = []
        for part, width in zip(parts, widths, strict=True):
            _, first_row, count = PARTS[part]
            lane = lax.broadcasted_iota(jnp.int32, (TOKM, width), 1)
            at_query.append(lane % count + first_row)
        at_query = jnp.concatenate(at_query, axis=1)
        of_key, of_query = jnp.zeros_like(at_key), jnp.zeros_like(at_query)
        end = jnp.zeros((1, 1), jnp.int32)
        for i in range(RESPS):
            end = end + seg_ref[micro : micro + 1, i : i + 1]
            of_key = of_key + (at_key >= end).astype(jnp.int32)
            of_query = of_query + (at_query >= end).astype(jnp.int32)
        allowed = (of_key == of_query) & (at_key <= at_query)
        near_mask = jnp.where(allowed, 0.0, -jnp.inf).astype(jnp.float32)

        outs = []
        for layer in range(2):
            is_own = second == layer

            def one_of_both(refs, block, is_own=is_own):
                own, other = (ref[block] for ref in refs)
                return jnp.where(is_own, own, other)

            x = []
            for g in range(KVH):
                query = []
                for part in parts:
                    query_refs = late_refs if part == len(PARTS) - 1 else (own_ref, other_ref)
                    query.append(one_of_both(query_refs, query_block(part, g)))
                query = jnp.concatenate(query, axis=1)
                if layer == 1:
                    query = query.astype(jnp.float32) + outs[0][g].astype(jnp.float32)
                elif carried_ref is not None:
                    query = query.astype(jnp.float32) + carried_ref[group_rows(g)].astype(jnp.float32)
                x.append(query.astype(jnp.bfloat16))

            def blocks(column, layer=layer, one_of_both=one_of_both):
                def of_group(g):
                    lanes = slice(column + g * HEAD_SIZE, column + (g + 1) * HEAD_SIZE)
                    rows, _ = near_block(micro, lanes.start // LANES)
                    inside = slice(lanes.start % LANES, lanes.start % LANES + HEAD_SIZE)
                    near = one_of_both((own_ref, other_ref), (rows, inside))
                    return [kv0_ref[layer, :, lanes], kv1_ref[layer, :, lanes], near]

                return of_group

            outs.append(attend(x, widths, blocks(0), blocks(KVW), near_mask, att_ref))
        return outs[1], [jnp.where(second == 0, *both) for both in zip(*outs, strict=True)]

    if not hopped:
        kv0_ref, kv1_ref, *out_refs, att_ref = refs

        @pl.when(pair == 0)
        def _():
            outs = both_layers(None, kv0_ref, kv1_ref, att_ref)
            first = 0
            for i, width in enumerate(widths):
                for ref, groups in zip(out_refs[2 * i : 2 * i + 2], outs, strict=True):
                    for g in range(KVH):
                        ref[group_rows(g)] = groups[g][:, first : first + width]
                first += width

        return

    carried_ref, kept_ref, *refs = refs
    ready_refs, refs = refs[:ready], refs[ready:]
    kv0_ref, kv1_ref, out_ref, att_ref, *own_copies = refs
    copies = []
    rows_ref = out_ref
    if own_copies:
        rows_ref, sems = own_copies
        first = 0
        for i, source in enumerate((*ready_refs, rows_ref)):
            here = out_ref.at[first : first + source.shape[0]]
            copies.append(pltpu.make_async_copy(source, here, sems.at[i]))
            first += source.shape[0]
        for copy in copies[:-1]:
            copy.start()

    def lay_out(groups):
        _, _, count = PARTS[parts[0]]
        for g in range(KVH):
            normed = groups[g].T
            for at in range(GROUP):
                h = g * GROUP + at
                rows_ref[:, h * HEAD_SIZE : (h + 1) * HEAD_SIZE] = normed[at * count : (at + 1) * count]

    @pl.when(pair == 0)
    def _():
        lay_out([kept_ref[group_rows(g)] for g in range(KVH)])

    @pl.when(pair != 0)
    def _():
        lay_out(both_layers(carried_ref, kv0_ref, kv1_ref, att_ref)[1])

    if copies:
        copies[-1].start()
        for copy in copies:
            copy.wait()


def attend_pair(parts, fixed, kv, carried=(), ready=()):
    vmem = pl.BlockSpec(memory_space=pltpu.VMEM)
    middle = [*carried, *ready]
    counts = [PARTS[part][2] for part in parts]
    count = sum(counts)
    scratch = [pltpu.VMEM((KVH, HEAD_SIZE, GROUP * count), jnp.float32)]
    shapes, out_specs = [(count, WIDTH)], [vmem]
    if not carried:
        shapes = [(KVH * HEAD_SIZE, GROUP * n) for n in counts for _ in range(2)]
        out_specs = [vmem] * len(shapes)
    elif ready:
        shapes, out_specs = [(MB * TOKM, WIDTH)], [pl.BlockSpec(memory_space=pl.ANY)]
        scratch += [pltpu.VMEM((count, WIDTH), jnp.bfloat16), pltpu.SemaphoreType.DMA((len(PARTS),))]
    return pl.pallas_call(
        functools.partial(pair_kernel, parts, bool(carried), len(ready)),
        out_shape=[jax.ShapeDtypeStruct(shape, jnp.bfloat16) for shape in shapes],
        in_specs=[vmem] * (len(fixed) + len(middle) + len(kv)),
        out_specs=out_specs,
        scratch_shapes=scratch,
        compiler_params=pltpu.CompilerParams(vmem_limit_bytes=12 * 1024 * 1024),
        cost_estimate=pl.CostEstimate(
            flops=1_600_000_000 + 50_000_000 * count,
            bytes_accessed=4 * 1024 * 1024,
            transcendentals=2 * HQ * count * (PLEN + TOKM),
        ),
    )(*fixed, *middle, *kv)


def spread_prefix(prefix, is_owner, is_other_core, beside):
    half = PLEN // 2
    parts = math.prod(lax.axis_size(axis) for axis in PLANE)
    arrived = swap(prefix[half:], "c")
    zero = jnp.zeros((), jnp.bfloat16)
    mine = jnp.where(is_owner, prefix[:half], jnp.where(is_other_core, arrived, zero))
    pieces = lax.all_to_all(mine.reshape(parts, half // parts, -1), PLANE, 0, 0)
    piece = jnp.sum(pieces, axis=0)
    piece = piece + swap(piece, "zh")
    piece, beside = lax.optimization_barrier((piece, beside))
    copies = lax.axis_size("yl") * parts
    gathered = lax.all_to_all(jnp.broadcast_to(piece[None], (copies, *piece.shape)), SPREAD, 0, 0)
    gathered = gathered.reshape(lax.axis_size("yl"), -1, gathered.shape[2])
    return gathered, swap(gathered, "c"), beside


def local(queries, resp_kv, prefix_kv, owner, seg_len):
    at = {axis: lax.axis_index(axis) for axis in RESP}
    place = jnp.int32(0)
    for axis in RESP:
        place = place * lax.axis_size(axis) + at[axis]
    owner_here = lax.dynamic_index_in_dim(owner[0], at["p"], 0, keepdims=False)

    early, late = packed(queries[0], resp_kv[0])
    *kv, early_other = spread_prefix(
        prefix_kv[0], owner_here == place, owner_here == (place ^ 1), swap(early, "yl")
    )

    fixed = [(seg_len, early, early_other)]
    fixed += [(*fixed[0], late, swap(late, "yl"))] * (len(PARTS) - 1)
    parts = range(len(PARTS))
    carried = []
    for micro in range(MB):
        together = tuple(i for i in parts if PARTS[i][0] == micro)
        outs = attend_pair(together, fixed[together[0]], kv)
        for last, kept in zip(outs[::2], outs[1::2], strict=True):
            carried.append((lax.ppermute(last, SECTION, [(0, 3), (1, 2)]), kept))
    ready = []
    for i in parts[:-1]:
        ready += attend_pair((i,), fixed[i], kv, carried[i])
        ready[i], carried[i + 1] = lax.optimization_barrier((ready[i], carried[i + 1]))
    return attend_pair((parts[-1],), fixed[-1], kv, carried[-1], ready)[0][None]


def solution(mesh):
    fine = Mesh(mesh.devices.reshape(2, 2, PROMPTS, 2, 2, 4, 2), SECTION + RESP)
    return jax.shard_map(
        local,
        mesh=fine,
        in_specs=(
            P(SECTION, RESP, None),
            P(SECTION, RESP, None),
            P(SECTION, RESP, None),
            P(SECTION, None),
            P(RESP, None),
        ),
        out_specs=P(SECTION, RESP, None),
        check_vma=False,
    )
```

```python
import functools
import math

import jax
import jax.numpy as jnp
from jax import lax
from jax.experimental import pallas as pl
from jax.experimental.pallas import tpu as pltpu
from jax.sharding import Mesh, PartitionSpec as P

HQ = 32
KVH = 4
GROUP = HQ // KVH
HEAD_SIZE = 128
WIDTH = HQ * HEAD_SIZE
KVW = KVH * HEAD_SIZE
PLEN = 512
TOKM = 32
MB = 2
LANES = GROUP * TOKM
CHUNKS = 2 * KVW // LANES
PARTS = ((0, 0, 32), (1, 0, 16), (1, 16, 16))
RESPS = 4
PROMPTS = 4
EPS = 1e-06
EXP2_SCALE = math.log2(math.e) / math.sqrt(HEAD_SIZE)

SECTION = ("yh", "yl")
RESP = ("p", "zh", "zl", "x", "c")
PLANE = ("x", "zl")
SPREAD = ("yl", *PLANE)


def swap(x, axis):
    return lax.ppermute(x, axis, [(0, 1), (1, 0)])


def product(a, b, a_over, b_over):
    over = (((a_over,), (b_over,)), ((), ()))
    return lax.dot_general(a, b, over, preferred_element_type=jnp.float32)


def over_rows(reduce, blocks):
    pair = jnp.maximum if reduce is jnp.max else jnp.add
    wide = reduce(pair(blocks[0], blocks[1]), axis=0, keepdims=True)
    return pair(wide, reduce(blocks[2], axis=0, keepdims=True))


def over_heads(total, widths):
    sums, first = [], 0
    for width in widths:
        part = total[:, first : first + width]
        reach = width // GROUP
        while reach < width:
            part = part + pltpu.roll(part, reach, 1)
            reach *= 2
        sums.append(part)
        first += width
    return jnp.concatenate(sums, axis=1)


def attend(x, widths, keys, values, near_mask, att_ref):
    groups = range(KVH)
    lanes = x[0].shape[1]
    scores = [[product(k, x[g], 1, 0) for k in keys(g)] for g in groups]
    for g in groups:
        scores[g][2] = scores[g][2] + near_mask
    top = [over_rows(jnp.max, scores[g]) for g in groups]
    raised = [[jnp.exp2((s - top[g]) * EXP2_SCALE) for s in scores[g]] for g in groups]
    share = [1.0 / over_rows(jnp.sum, raised[g]) for g in groups]
    weights = [[(e * share[g]).astype(jnp.bfloat16) for e in raised[g]] for g in groups]
    total = jnp.zeros((1, lanes), jnp.float32)
    for g in groups:
        out = sum(product(v, w, 0, 0) for v, w in zip(values(g), weights[g], strict=True))
        att_ref[g] = out
        total = total + jnp.sum(out * out, axis=0, keepdims=True)
    scaling = lax.rsqrt(over_heads(total, widths) * (1.0 / WIDTH) + EPS)
    return [(att_ref[g] * scaling).astype(jnp.bfloat16) for g in groups]


def pack_kernel(q_ref, rkv_ref, early_ref, late_ref):
    for part, (micro, first, count) in enumerate(PARTS):
        out_ref = late_ref if part == len(PARTS) - 1 else early_ref
        rows = pl.ds(micro * TOKM + first, count)
        for g in range(KVH):
            heads = [
                q_ref[rows, h * HEAD_SIZE : (h + 1) * HEAD_SIZE]
                for h in range(g * GROUP, (g + 1) * GROUP)
            ]
            out_ref[query_block(part, g)] = jnp.concatenate(heads, axis=0).T
    for micro in range(MB):
        rows = pl.ds(micro * TOKM, TOKM)
        for chunk in range(CHUNKS):
            early_ref[near_block(micro, chunk)] = rkv_ref[rows, chunk * LANES : (chunk + 1) * LANES]


def query_block(part, g):
    lanes = GROUP * PARTS[part][2]
    beside = LANES // lanes
    first = 0
    if part < len(PARTS) - 1:
        first = sum(KVH * GROUP * count * HEAD_SIZE // LANES for _, _, count in PARTS[:part])
    first += g // beside * HEAD_SIZE
    lane = g % beside * lanes
    return slice(first, first + HEAD_SIZE), slice(lane, lane + lanes)


def near_block(micro, chunk):
    first = query_block(len(PARTS) - 2, KVH - 1)[0].stop + (micro * CHUNKS + chunk) * TOKM
    return slice(first, first + TOKM), slice(None)


def packed(q, rkv):
    vmem = pl.BlockSpec(memory_space=pltpu.VMEM)
    sizes = near_block(MB - 1, CHUNKS - 1)[0].stop, query_block(len(PARTS) - 1, KVH - 1)[0].stop
    return pl.pallas_call(
        pack_kernel,
        out_shape=tuple(jax.ShapeDtypeStruct((size, LANES), jnp.bfloat16) for size in sizes),
        in_specs=[vmem, vmem],
        out_specs=(vmem, vmem),
        compiler_params=pltpu.CompilerParams(vmem_limit_bytes=12 * 1024 * 1024),
        cost_estimate=pl.CostEstimate(flops=0, bytes_accessed=1280 * 1024, transcendentals=0),
    )(q, rkv)


def pair_kernel(parts, hopped, ready, seg_ref, own_ref, other_ref, *refs):
    micro = PARTS[parts[0]][0]
    widths = [GROUP * PARTS[part][2] for part in parts]
    late_refs = ()
    if micro > 0:
        late_refs, refs = refs[:2], refs[2:]
    second, pair = lax.axis_index("yl"), lax.axis_index("yh")

    def group_rows(g):
        return slice(g * HEAD_SIZE, (g + 1) * HEAD_SIZE)

    def both_layers(carried_ref, kv0_ref, kv1_ref, att_ref):
        at_key = lax.broadcasted_iota(jnp.int32, (TOKM, sum(widths)), 0)
        at_query = []
        for part, width in zip(parts, widths, strict=True):
            _, first_row, count = PARTS[part]
            lane = lax.broadcasted_iota(jnp.int32, (TOKM, width), 1)
            at_query.append(lane % count + first_row)
        at_query = jnp.concatenate(at_query, axis=1)
        of_key, of_query = jnp.zeros_like(at_key), jnp.zeros_like(at_query)
        end = jnp.zeros((1, 1), jnp.int32)
        for i in range(RESPS):
            end = end + seg_ref[micro : micro + 1, i : i + 1]
            of_key = of_key + (at_key >= end).astype(jnp.int32)
            of_query = of_query + (at_query >= end).astype(jnp.int32)
        allowed = (of_key == of_query) & (at_key <= at_query)
        near_mask = jnp.where(allowed, 0.0, -jnp.inf).astype(jnp.float32)

        outs = []
        for layer in range(2):
            is_own = second == layer

            def one_of_both(refs, block, is_own=is_own):
                own, other = (ref[block] for ref in refs)
                return jnp.where(is_own, own, other)

            x = []
            for g in range(KVH):
                query = []
                for part in parts:
                    query_refs = late_refs if part == len(PARTS) - 1 else (own_ref, other_ref)
                    query.append(one_of_both(query_refs, query_block(part, g)))
                query = jnp.concatenate(query, axis=1)
                if layer == 1:
                    query = query.astype(jnp.float32) + outs[0][g].astype(jnp.float32)
                elif carried_ref is not None:
                    query = query.astype(jnp.float32) + carried_ref[group_rows(g)].astype(jnp.float32)
                x.append(query.astype(jnp.bfloat16))

            def blocks(column, layer=layer, one_of_both=one_of_both):
                def of_group(g):
                    lanes = slice(column + g * HEAD_SIZE, column + (g + 1) * HEAD_SIZE)
                    rows, _ = near_block(micro, lanes.start // LANES)
                    inside = slice(lanes.start % LANES, lanes.start % LANES + HEAD_SIZE)
                    near = one_of_both((own_ref, other_ref), (rows, inside))
                    return [kv0_ref[layer, :, lanes], kv1_ref[layer, :, lanes], near]

                return of_group

            outs.append(attend(x, widths, blocks(0), blocks(KVW), near_mask, att_ref))
        return outs[1], [jnp.where(second == 0, *both) for both in zip(*outs, strict=True)]

    if not hopped:
        kv0_ref, kv1_ref, *out_refs, att_ref = refs

        @pl.when(pair == 0)
        def _():
            outs = both_layers(None, kv0_ref, kv1_ref, att_ref)
            first = 0
            for i, width in enumerate(widths):
                for ref, groups in zip(out_refs[2 * i : 2 * i + 2], outs, strict=True):
                    for g in range(KVH):
                        ref[group_rows(g)] = groups[g][:, first : first + width]
                first += width

        return

    carried_ref, kept_ref, *refs = refs
    ready_refs, refs = refs[:ready], refs[ready:]
    kv0_ref, kv1_ref, out_ref, att_ref, *own_copies = refs
    copies = []
    rows_ref = out_ref
    if own_copies:
        rows_ref, sems = own_copies
        first = 0
        for i, source in enumerate((*ready_refs, rows_ref)):
            here = out_ref.at[first : first + source.shape[0]]
            copies.append(pltpu.make_async_copy(source, here, sems.at[i]))
            first += source.shape[0]
        for copy in copies[:-1]:
            copy.start()

    def lay_out(groups):
        _, _, count = PARTS[parts[0]]
        for g in range(KVH):
            normed = groups[g].T
            for at in range(GROUP):
                h = g * GROUP + at
                rows_ref[:, h * HEAD_SIZE : (h + 1) * HEAD_SIZE] = normed[at * count : (at + 1) * count]

    @pl.when(pair == 0)
    def _():
        lay_out([kept_ref[group_rows(g)] for g in range(KVH)])

    @pl.when(pair != 0)
    def _():
        lay_out(both_layers(carried_ref, kv0_ref, kv1_ref, att_ref)[1])

    if copies:
        copies[-1].start()
        for copy in copies:
            copy.wait()


def attend_pair(parts, fixed, kv, carried=(), ready=()):
    vmem = pl.BlockSpec(memory_space=pltpu.VMEM)
    middle = [*carried, *ready]
    counts = [PARTS[part][2] for part in parts]
    count = sum(counts)
    scratch = [pltpu.VMEM((KVH, HEAD_SIZE, GROUP * count), jnp.float32)]
    shapes, out_specs = [(count, WIDTH)], [vmem]
    if not carried:
        shapes = [(KVH * HEAD_SIZE, GROUP * n) for n in counts for _ in range(2)]
        out_specs = [vmem] * len(shapes)
    elif ready:
        shapes, out_specs = [(MB * TOKM, WIDTH)], [pl.BlockSpec(memory_space=pl.ANY)]
        scratch += [pltpu.VMEM((count, WIDTH), jnp.bfloat16), pltpu.SemaphoreType.DMA((len(PARTS),))]
    return pl.pallas_call(
        functools.partial(pair_kernel, parts, bool(carried), len(ready)),
        out_shape=[jax.ShapeDtypeStruct(shape, jnp.bfloat16) for shape in shapes],
        in_specs=[vmem] * (len(fixed) + len(middle) + len(kv)),
        out_specs=out_specs,
        scratch_shapes=scratch,
        compiler_params=pltpu.CompilerParams(vmem_limit_bytes=12 * 1024 * 1024),
        cost_estimate=pl.CostEstimate(
            flops=1_600_000_000 + 50_000_000 * count,
            bytes_accessed=4 * 1024 * 1024,
            transcendentals=2 * HQ * count * (PLEN + TOKM),
        ),
    )(*fixed, *middle, *kv)


def spread_prefix(prefix, is_owner, is_other_core, beside):
    half = PLEN // 2
    parts = math.prod(lax.axis_size(axis) for axis in PLANE)
    arrived = swap(prefix[half:], "c")
    zero = jnp.zeros((), jnp.bfloat16)
    mine = jnp.where(is_owner, prefix[:half], jnp.where(is_other_core, arrived, zero))
    pieces = lax.all_to_all(mine.reshape(parts, half // parts, -1), PLANE, 0, 0)
    piece = jnp.sum(pieces, axis=0)
    piece = piece + swap(piece, "zh")
    piece, beside = lax.optimization_barrier((piece, beside))
    copies = lax.axis_size("yl") * parts
    gathered = lax.all_to_all(jnp.broadcast_to(piece[None], (copies, *piece.shape)), SPREAD, 0, 0)
    gathered = gathered.reshape(lax.axis_size("yl"), -1, gathered.shape[2])
    return gathered, swap(gathered, "c"), beside


def local(queries, resp_kv, prefix_kv, owner, seg_len):
    at = {axis: lax.axis_index(axis) for axis in RESP}
    place = jnp.int32(0)
    for axis in RESP:
        place = place * lax.axis_size(axis) + at[axis]
    owner_here = lax.dynamic_index_in_dim(owner[0], at["p"], 0, keepdims=False)

    early, late = packed(queries[0], resp_kv[0])
    *kv, early_other = spread_prefix(
        prefix_kv[0], owner_here == place, owner_here == (place ^ 1), swap(early, "yl")
    )

    fixed = [(seg_len, early, early_other)]
    fixed += [(*fixed[0], late, swap(late, "yl"))] * (len(PARTS) - 1)
    parts = range(len(PARTS))
    carried = []
    for micro in range(MB):
        together = tuple(i for i in parts if PARTS[i][0] == micro)
        outs = attend_pair(together, fixed[together[0]], kv)
        for last, kept in zip(outs[::2], outs[1::2], strict=True):
            carried.append((lax.ppermute(last, SECTION, [(0, 3), (1, 2)]), kept))
    ready = []
    for i in parts[:-1]:
        ready += attend_pair((i,), fixed[i], kv, carried[i])
        ready[i], carried[i + 1] = lax.optimization_barrier((ready[i], carried[i + 1]))
    return attend_pair((parts[-1],), fixed[-1], kv, carried[-1], ready)[0][None]


def solution(mesh):
    fine = Mesh(mesh.devices.reshape(2, 2, PROMPTS, 2, 2, 4, 2), SECTION + RESP)
    return jax.shard_map(
        local,
        mesh=fine,
        in_specs=(
            P(SECTION, RESP, None),
            P(SECTION, RESP, None),
            P(SECTION, RESP, None),
            P(SECTION, None),
            P(RESP, None),
        ),
        out_specs=P(SECTION, RESP, None),
        check_vma=False,
    )
```

```python
import functools
import math

import jax
import jax.numpy as jnp
from jax import lax
from jax.experimental import pallas as pl
from jax.experimental.pallas import tpu as pltpu
from jax.sharding import Mesh, PartitionSpec as P

HQ = 32
KVH = 4
GROUP = HQ // KVH
HEAD_SIZE = 128
WIDTH = HQ * HEAD_SIZE
KVW = KVH * HEAD_SIZE
PLEN = 512
TOKM = 32
MB = 2
LANES = GROUP * TOKM
CHUNKS = 2 * KVW // LANES
PARTS = ((0, 0, 32), (1, 0, 16), (1, 16, 16))
RESPS = 4
PROMPTS = 4
EPS = 1e-06
EXP2_SCALE = math.log2(math.e) / math.sqrt(HEAD_SIZE)

SECTION = ("yh", "yl")
RESP = ("p", "zh", "zl", "x", "c")
PLANE = ("zl", "x")
SPREAD = ("yl", "x", "zl")


def swap(x, axis):
    return lax.ppermute(x, axis, [(0, 1), (1, 0)])


def product(a, b, a_over, b_over):
    over = (((a_over,), (b_over,)), ((), ()))
    return lax.dot_general(a, b, over, preferred_element_type=jnp.float32)


def over_rows(reduce, blocks):
    pair = jnp.maximum if reduce is jnp.max else jnp.add
    wide = reduce(pair(blocks[0], blocks[1]), axis=0, keepdims=True)
    return pair(wide, reduce(blocks[2], axis=0, keepdims=True))


def over_heads(total, widths):
    sums, first = [], 0
    for width in widths:
        part = total[:, first : first + width]
        reach = width // GROUP
        while reach < width:
            part = part + pltpu.roll(part, reach, 1)
            reach *= 2
        sums.append(part)
        first += width
    return jnp.concatenate(sums, axis=1)


def attend(x, widths, keys, values, near_mask, att_ref):
    groups = range(KVH)
    lanes = x[0].shape[1]
    scores = [[product(k, x[g], 1, 0) for k in keys(g)] for g in groups]
    for g in groups:
        scores[g][2] = scores[g][2] + near_mask
    top = [over_rows(jnp.max, scores[g]) for g in groups]
    raised = [[jnp.exp2((s - top[g]) * EXP2_SCALE) for s in scores[g]] for g in groups]
    share = [1.0 / over_rows(jnp.sum, raised[g]) for g in groups]
    weights = [[(e * share[g]).astype(jnp.bfloat16) for e in raised[g]] for g in groups]
    total = jnp.zeros((1, lanes), jnp.float32)
    for g in groups:
        out = sum(product(v, w, 0, 0) for v, w in zip(values(g), weights[g], strict=True))
        att_ref[g] = out
        total = total + jnp.sum(out * out, axis=0, keepdims=True)
    scaling = lax.rsqrt(over_heads(total, widths) * (1.0 / WIDTH) + EPS)
    return [(att_ref[g] * scaling).astype(jnp.bfloat16) for g in groups]


def pack_kernel(q_ref, rkv_ref, early_ref, late_ref):
    for part, (micro, first, count) in enumerate(PARTS):
        out_ref = late_ref if part == len(PARTS) - 1 else early_ref
        rows = pl.ds(micro * TOKM + first, count)
        for g in range(KVH):
            heads = [
                q_ref[rows, h * HEAD_SIZE : (h + 1) * HEAD_SIZE]
                for h in range(g * GROUP, (g + 1) * GROUP)
            ]
            out_ref[query_block(part, g)] = jnp.concatenate(heads, axis=0).T
    for micro in range(MB):
        rows = pl.ds(micro * TOKM, TOKM)
        for chunk in range(CHUNKS):
            early_ref[near_block(micro, chunk)] = rkv_ref[rows, chunk * LANES : (chunk + 1) * LANES]


def query_block(part, g):
    lanes = GROUP * PARTS[part][2]
    beside = LANES // lanes
    first = 0
    if part < len(PARTS) - 1:
        first = sum(KVH * GROUP * count * HEAD_SIZE // LANES for _, _, count in PARTS[:part])
    first += g // beside * HEAD_SIZE
    lane = g % beside * lanes
    return slice(first, first + HEAD_SIZE), slice(lane, lane + lanes)


def near_block(micro, chunk):
    first = query_block(len(PARTS) - 2, KVH - 1)[0].stop + (micro * CHUNKS + chunk) * TOKM
    return slice(first, first + TOKM), slice(None)


def packed(q, rkv):
    vmem = pl.BlockSpec(memory_space=pltpu.VMEM)
    sizes = near_block(MB - 1, CHUNKS - 1)[0].stop, query_block(len(PARTS) - 1, KVH - 1)[0].stop
    return pl.pallas_call(
        pack_kernel,
        out_shape=tuple(jax.ShapeDtypeStruct((size, LANES), jnp.bfloat16) for size in sizes),
        in_specs=[vmem, vmem],
        out_specs=(vmem, vmem),
        compiler_params=pltpu.CompilerParams(vmem_limit_bytes=12 * 1024 * 1024),
        cost_estimate=pl.CostEstimate(flops=0, bytes_accessed=1280 * 1024, transcendentals=0),
    )(q, rkv)


def pair_kernel(parts, hopped, ready, seg_ref, own_ref, other_ref, *refs):
    micro = PARTS[parts[0]][0]
    widths = [GROUP * PARTS[part][2] for part in parts]
    late_refs = ()
    if micro > 0:
        late_refs, refs = refs[:2], refs[2:]
    second, pair = lax.axis_index("yl"), lax.axis_index("yh")

    def group_rows(g):
        return slice(g * HEAD_SIZE, (g + 1) * HEAD_SIZE)

    def both_layers(carried_ref, kv0_ref, kv1_ref, att_ref):
        at_key = lax.broadcasted_iota(jnp.int32, (TOKM, sum(widths)), 0)
        at_query = []
        for part, width in zip(parts, widths, strict=True):
            _, first_row, count = PARTS[part]
            lane = lax.broadcasted_iota(jnp.int32, (TOKM, width), 1)
            at_query.append(lane % count + first_row)
        at_query = jnp.concatenate(at_query, axis=1)
        of_key, of_query = jnp.zeros_like(at_key), jnp.zeros_like(at_query)
        end = jnp.zeros((1, 1), jnp.int32)
        for i in range(RESPS):
            end = end + seg_ref[micro : micro + 1, i : i + 1]
            of_key = of_key + (at_key >= end).astype(jnp.int32)
            of_query = of_query + (at_query >= end).astype(jnp.int32)
        allowed = (of_key == of_query) & (at_key <= at_query)
        near_mask = jnp.where(allowed, 0.0, -jnp.inf).astype(jnp.float32)

        outs = []
        for layer in range(2):
            is_own = second == layer

            def one_of_both(refs, block, is_own=is_own):
                own, other = (ref[block] for ref in refs)
                return jnp.where(is_own, own, other)

            x = []
            for g in range(KVH):
                query = []
                for part in parts:
                    query_refs = late_refs if part == len(PARTS) - 1 else (own_ref, other_ref)
                    query.append(one_of_both(query_refs, query_block(part, g)))
                query = jnp.concatenate(query, axis=1)
                if layer == 1:
                    query = query.astype(jnp.float32) + outs[0][g].astype(jnp.float32)
                elif carried_ref is not None:
                    query = query.astype(jnp.float32) + carried_ref[group_rows(g)].astype(jnp.float32)
                x.append(query.astype(jnp.bfloat16))

            def blocks(column, layer=layer, one_of_both=one_of_both):
                def of_group(g):
                    lanes = slice(column + g * HEAD_SIZE, column + (g + 1) * HEAD_SIZE)
                    rows, _ = near_block(micro, lanes.start // LANES)
                    inside = slice(lanes.start % LANES, lanes.start % LANES + HEAD_SIZE)
                    near = one_of_both((own_ref, other_ref), (rows, inside))
                    return [kv0_ref[layer, :, lanes], kv1_ref[layer, :, lanes], near]

                return of_group

            outs.append(attend(x, widths, blocks(0), blocks(KVW), near_mask, att_ref))
        return outs[1], [jnp.where(second == 0, *both) for both in zip(*outs, strict=True)]

    if not hopped:
        kv0_ref, kv1_ref, *out_refs, att_ref = refs

        @pl.when(pair == 0)
        def _():
            outs = both_layers(None, kv0_ref, kv1_ref, att_ref)
            first = 0
            for i, width in enumerate(widths):
                for ref, groups in zip(out_refs[2 * i : 2 * i + 2], outs, strict=True):
                    for g in range(KVH):
                        ref[group_rows(g)] = groups[g][:, first : first + width]
                first += width

        return

    carried_ref, kept_ref, *refs = refs
    ready_refs, refs = refs[:ready], refs[ready:]
    kv0_ref, kv1_ref, out_ref, att_ref, *own_copies = refs
    copies = []
    rows_ref = out_ref
    if own_copies:
        rows_ref, sems = own_copies
        first = 0
        for i, source in enumerate((*ready_refs, rows_ref)):
            here = out_ref.at[first : first + source.shape[0]]
            copies.append(pltpu.make_async_copy(source, here, sems.at[i]))
            first += source.shape[0]
        for copy in copies[:-1]:
            copy.start()

    def lay_out(groups):
        _, _, count = PARTS[parts[0]]
        for g in range(KVH):
            normed = groups[g].T
            for at in range(GROUP):
                h = g * GROUP + at
                rows_ref[:, h * HEAD_SIZE : (h + 1) * HEAD_SIZE] = normed[at * count : (at + 1) * count]

    @pl.when(pair == 0)
    def _():
        lay_out([kept_ref[group_rows(g)] for g in range(KVH)])

    @pl.when(pair != 0)
    def _():
        lay_out(both_layers(carried_ref, kv0_ref, kv1_ref, att_ref)[1])

    if copies:
        copies[-1].start()
        for copy in copies:
            copy.wait()


def attend_pair(parts, fixed, kv, carried=(), ready=()):
    vmem = pl.BlockSpec(memory_space=pltpu.VMEM)
    middle = [*carried, *ready]
    counts = [PARTS[part][2] for part in parts]
    count = sum(counts)
    scratch = [pltpu.VMEM((KVH, HEAD_SIZE, GROUP * count), jnp.float32)]
    shapes, out_specs = [(count, WIDTH)], [vmem]
    if not carried:
        shapes = [(KVH * HEAD_SIZE, GROUP * n) for n in counts for _ in range(2)]
        out_specs = [vmem] * len(shapes)
    elif ready:
        shapes, out_specs = [(MB * TOKM, WIDTH)], [pl.BlockSpec(memory_space=pl.ANY)]
        scratch += [pltpu.VMEM((count, WIDTH), jnp.bfloat16), pltpu.SemaphoreType.DMA((len(PARTS),))]
    return pl.pallas_call(
        functools.partial(pair_kernel, parts, bool(carried), len(ready)),
        out_shape=[jax.ShapeDtypeStruct(shape, jnp.bfloat16) for shape in shapes],
        in_specs=[vmem] * (len(fixed) + len(middle) + len(kv)),
        out_specs=out_specs,
        scratch_shapes=scratch,
        compiler_params=pltpu.CompilerParams(vmem_limit_bytes=12 * 1024 * 1024),
        cost_estimate=pl.CostEstimate(
            flops=1_600_000_000 + 50_000_000 * count,
            bytes_accessed=4 * 1024 * 1024,
            transcendentals=2 * HQ * count * (PLEN + TOKM),
        ),
    )(*fixed, *middle, *kv)


def spread_prefix(prefix, is_owner, is_other_core, beside):
    half = PLEN // 2
    parts = math.prod(lax.axis_size(axis) for axis in PLANE)
    arrived = swap(prefix[half:], "c")
    zero = jnp.zeros((), jnp.bfloat16)
    mine = jnp.where(is_owner, prefix[:half], jnp.where(is_other_core, arrived, zero))
    pieces = lax.all_to_all(mine.reshape(parts, half // parts, -1), PLANE, 0, 0)
    piece = jnp.sum(pieces, axis=0)
    piece = piece + swap(piece, "zh")
    piece, beside = lax.optimization_barrier((piece, beside))
    copies = lax.axis_size("yl") * parts
    gathered = lax.all_to_all(jnp.broadcast_to(piece[None], (copies, *piece.shape)), SPREAD, 0, 0)
    gathered = gathered.reshape(lax.axis_size("yl"), -1, gathered.shape[2])
    return gathered, swap(gathered, "c"), beside


def local(queries, resp_kv, prefix_kv, owner, seg_len):
    at = {axis: lax.axis_index(axis) for axis in RESP}
    place = jnp.int32(0)
    for axis in RESP:
        place = place * lax.axis_size(axis) + at[axis]
    owner_here = lax.dynamic_index_in_dim(owner[0], at["p"], 0, keepdims=False)

    early, late = packed(queries[0], resp_kv[0])
    *kv, early_other = spread_prefix(
        prefix_kv[0], owner_here == place, owner_here == (place ^ 1), swap(early, "yl")
    )

    fixed = [(seg_len, early, early_other)]
    fixed += [(*fixed[0], late, swap(late, "yl"))] * (len(PARTS) - 1)
    parts = range(len(PARTS))
    carried = []
    for micro in range(MB):
        together = tuple(i for i in parts if PARTS[i][0] == micro)
        outs = attend_pair(together, fixed[together[0]], kv)
        for last, kept in zip(outs[::2], outs[1::2], strict=True):
            carried.append((lax.ppermute(last, SECTION, [(0, 3), (1, 2)]), kept))
    ready = []
    for i in parts[:-1]:
        ready += attend_pair((i,), fixed[i], kv, carried[i])
        ready[i], carried[i + 1] = lax.optimization_barrier((ready[i], carried[i + 1]))
    return attend_pair((parts[-1],), fixed[-1], kv, carried[-1], ready)[0][None]


def solution(mesh):
    fine = Mesh(mesh.devices.reshape(2, 2, PROMPTS, 2, 2, 4, 2), SECTION + RESP)
    return jax.shard_map(
        local,
        mesh=fine,
        in_specs=(
            P(SECTION, RESP, None),
            P(SECTION, RESP, None),
            P(SECTION, RESP, None),
            P(SECTION, None),
            P(RESP, None),
        ),
        out_specs=P(SECTION, RESP, None),
        check_vma=False,
    )
```
